256 devices in a mesh: row: 16 (over x, y_lo, core), col: 16 (over y_hi, z).
Axes of the slice: x: 4, y: 4 (y_hi: 2, y_lo: 2; y = y_hi * 2 + y_lo), z: 8, core: 2. Of those that a mesh axis runs over, the one named last changes fastest.
Arguments:
- pair: bfloat16 [512, 512, 128], P('row', 'col'), may hold values from -6 to 6
- gain_in: float32 [128], replicated, may hold values from 0.1 to 1.9
- in_weight: bfloat16 [128, 640], replicated, may hold values from -0.5 to 0.5
- gain_out: float32 [128], replicated, may hold values from 0.1 to 1.9
- out_weight: bfloat16 [128, 128], replicated, may hold values from -0.5 to 0.5
- out_grad: bfloat16 [512, 512, 128], P('row', 'col'), may hold values from -6 to 6
Outputs:
- update: bfloat16 [512, 512, 128], P('row', 'col')
- pair_grad: float32 [512, 512, 128], P('row', 'col')
- in_weight_grad: float32 [128, 640], replicated
- out_weight_grad: float32 [128, 128], replicated
- gain_grad: float32 [2, 128], replicated
The draws below stay inside these ranges and needn't reach their ends.
All inputs are finite; a program needn't handle non-finite values.
Results may differ from the reference program's by a relative error of at most 0.017.
Values may be sent and summed in bfloat16 or wider, within the bound.
A program may use at most 128 MiB of HBM per device.

```python
import jax
import jax.numpy as jnp
from jax import lax

PAIR_CH = 128
RESIDUES = 512


def block_scale(key, extent, pieces, smallest, high):
    def one(position, blocks):
        heights = jax.random.uniform(jax.random.fold_in(jax.random.fold_in(key, 6), position), (blocks,), jnp.float32, smallest / len(pieces), high / len(pieces))
        return jnp.repeat(jnp.exp(heights), extent[position] // blocks).reshape((-1,) + (1,) * (len(extent) - position - 1))

    level = one(*pieces[0])
    for cut in pieces[1:]:
        level = level * one(*cut)
    return level


def bell_draw(key, extent, scale, reach, shards=(), kind=jnp.bfloat16):
    array = scale * jax.random.normal(key, extent, jnp.float32)
    if shards:
        array = array * block_scale(key, extent, shards, -0.22, 0.18)
    return jnp.clip(array, -reach, reach).astype(kind)


def setup_inputs(seed: int = 0) -> dict:
    streams_of = jax.random.split(jax.random.key(seed), 7)
    pair = bell_draw(streams_of[0], (RESIDUES, RESIDUES, PAIR_CH), 1.0, 6.0, ((0, 16), (1, 16)))
    gain_in = jnp.clip(1.0 + 0.18 * jax.random.normal(streams_of[1], (PAIR_CH,), jnp.float32), 0.1, 1.9)
    in_weight = bell_draw(streams_of[2], (PAIR_CH, 5 * PAIR_CH), PAIR_CH ** -0.5, 0.5)
    gain_out = jnp.clip(1.0 + 0.18 * jax.random.normal(streams_of[3], (PAIR_CH,), jnp.float32), 0.1, 1.9)
    out_weight = bell_draw(streams_of[4], (PAIR_CH, PAIR_CH), PAIR_CH ** -0.5, 0.5)
    out_grad = bell_draw(streams_of[5], (RESIDUES, RESIDUES, PAIR_CH), 1.0, 6.0, ((0, 16), (1, 16)))
    return dict(pair=pair, gain_in=gain_in, in_weight=in_weight, gain_out=gain_out, out_weight=out_weight, out_grad=out_grad)


epsilon = 1e-05

def layer_norm(values, gain):
    average = lax.optimization_barrier(jnp.mean(values, axis=-1, keepdims=True))
    centred = values - average
    variance = lax.optimization_barrier(jnp.mean(centred * centred, axis=-1, keepdims=True))
    return centred * lax.rsqrt(variance + epsilon) * gain

def edge_gates(projected):
    width = projected.shape[-1] // 5
    parts = [projected[:, index * width:(index + 1) * width] for index in range(5)]
    left_edge = jax.nn.sigmoid(parts[0]) * parts[1]
    right_edge = jax.nn.sigmoid(parts[2]) * parts[3]
    gate_value = jax.nn.sigmoid(parts[4])
    return (left_edge, right_edge, gate_value)

def reference(pair, gain_in, in_weight, gain_out, out_weight, out_grad):
    residues = pair.shape[0]
    channels = pair.shape[2]
    cells_in = pair.astype(jnp.float32).reshape(residues * residues, channels)
    normed_in, in_back = jax.vjp(layer_norm, cells_in, gain_in)
    normed_bf = normed_in.astype(jnp.bfloat16)
    projected = jnp.dot(normed_bf, in_weight, preferred_element_type=jnp.float32)
    left_edge, right_edge, gate_value = edge_gates(projected)
    left_bf = left_edge.astype(jnp.bfloat16).reshape(residues, residues, channels)
    right_bf = right_edge.astype(jnp.bfloat16).reshape(residues, residues, channels)
    mixed = jnp.einsum('ikc,jkc->ijc', left_bf.astype(jnp.float32), right_bf.astype(jnp.float32))
    cells_mixed = mixed.reshape(residues * residues, channels)
    normed_out, out_back = jax.vjp(layer_norm, cells_mixed, gain_out)
    normed_out_bf = normed_out.astype(jnp.bfloat16)
    projected_out = jnp.dot(normed_out_bf, out_weight, preferred_element_type=jnp.float32)
    update = (gate_value * projected_out).astype(jnp.bfloat16).reshape(residues, residues, channels)
    cotangent = out_grad.astype(jnp.float32).reshape(residues * residues, channels)
    grad_proj_out = (cotangent * gate_value).astype(jnp.bfloat16)
    grad_gate = cotangent * projected_out
    out_weight_grad = jnp.dot(normed_out_bf.T, grad_proj_out, preferred_element_type=jnp.float32)
    grad_normed_out = jnp.dot(grad_proj_out, out_weight.T, preferred_element_type=jnp.float32)
    grad_mixed, grad_gain_out = out_back(grad_normed_out)
    grad_mixed_bf = grad_mixed.astype(jnp.bfloat16).reshape(residues, residues, channels)
    grad_left = jnp.einsum('ijc,jkc->ikc', grad_mixed_bf.astype(jnp.float32), right_bf.astype(jnp.float32))
    grad_right = jnp.einsum('ijc,ikc->jkc', grad_mixed_bf.astype(jnp.float32), left_bf.astype(jnp.float32))
    gate_fn_out, gate_back = jax.vjp(edge_gates, projected)
    grad_projected = gate_back((grad_left.reshape(residues * residues, channels), grad_right.reshape(residues * residues, channels), grad_gate))[0]
    grad_projected_bf = grad_projected.astype(jnp.bfloat16)
    in_weight_grad = jnp.dot(normed_bf.T, grad_projected_bf, preferred_element_type=jnp.float32)
    grad_normed_in = jnp.dot(grad_projected_bf, in_weight.T, preferred_element_type=jnp.float32)
    pair_grad, grad_gain_in = in_back(grad_normed_in)
    gain_grad = jnp.stack([grad_gain_in, grad_gain_out])
    return (update, pair_grad.reshape(residues, residues, channels), in_weight_grad, out_weight_grad, gain_grad)
```

```python
import functools

import jax
import jax.numpy as jnp
from jax import lax
from jax.experimental import pallas as pl
from jax.experimental.pallas import tpu as pltpu
from jax.sharding import PartitionSpec as P

EPS = 1e-05
MESH = pl.DeviceIdType.MESH
F32 = jnp.float32
BF16 = jnp.bfloat16
NT = (((1,), (1,)), ((), ()))
TN = (((0,), (0,)), ((), ()))


def dot(a, b, dims=(((1,), (0,)), ((), ()))):
    return lax.dot_general(a, b, dims, preferred_element_type=F32)


def swap_blocks(tiles):
    shape = tiles[0].shape
    flat = [t.reshape(-1, 128) for t in tiles]
    lane = lax.broadcasted_iota(jnp.int32, flat[0].shape, 1)
    low = lane < 64
    even = (lane // 32) % 2 == 0
    half = [None] * 4
    for q in range(2):
        a, b = flat[q], flat[q + 2]
        half[q] = jnp.where(low, a, pltpu.roll(b, 64, 1))
        half[q + 2] = jnp.where(low, pltpu.roll(a, 64, 1), b)
    out = [None] * 4
    for q in (0, 2):
        a, b = half[q], half[q + 1]
        out[q] = jnp.where(even, a, pltpu.roll(b, 32, 1))
        out[q + 1] = jnp.where(even, pltpu.roll(a, 96, 1), b)
    return [t.reshape(shape) for t in out]


def kernel(
    pair, gain_in, weight, gain_out, out_weight, out_grad,
    update_o, pair_grad_o, weight_grad_o, out_weight_grad_o, gain_grad_o,
    wide, sb1, rb1, left32, right32, edges, sb2, rb2, sb3, rb3, grad_mat, grad_far, sb4, rb4,
    normed, hat_in, rstd_in, gates, grad_po, grad_no, og_t, grad_p, w_t, ow_t, g_in, g_out,
    part, part_far, s1, r1, s2, r2, final,
    send, recv, sib_send, sib_recv, red_send, red_recv,
):
    row, col = lax.axis_index("row"), lax.axis_index("col")
    core, rx = row % 2, row // 2
    me = rx * 16 + col
    sibling = (rx * 2 + 1 - core, col)
    barrier = pltpu.get_barrier_semaphore()

    def partner(t):
        r = (rx + t // 16) % 8
        c = (col + t % 16) % 16
        return r, c

    def greet(t, carry):
        r, c = partner(t)
        pl.semaphore_signal(barrier, inc=1, device_id=(r * 2 + core, c), device_id_type=MESH)
        return carry

    lax.fori_loop(1, 128, greet, 0)
    pl.semaphore_signal(barrier, inc=1, device_id=sibling, device_id_type=MESH)

    def exchange(source, target, slot, own_source, own_target):
        def one(t, carry):
            r, c = partner(t)
            pltpu.make_async_remote_copy(
                src_ref=source(r, c), dst_ref=target, send_sem=send.at[slot], recv_sem=recv.at[slot],
                device_id=(r * 2 + core, c), device_id_type=MESH,
            ).start()
            return carry

        lax.fori_loop(1, 128, one, 0)
        own_target[...] = own_source[...]

    def arrive(buffer, semaphore):
        view = buffer.at[pl.ds(0, 127)]
        pltpu.make_async_copy(view, view, semaphore).wait()

    def to_sibling(source, target, slot):
        return pltpu.make_async_remote_copy(
            src_ref=source, dst_ref=target, send_sem=sib_send.at[slot], recv_sem=sib_recv.at[slot],
            device_id=sibling, device_id_type=MESH,
        )

    w_t[...] = weight[...].astype(F32).T.astype(BF16)
    g_in[...] = jnp.broadcast_to(gain_in[...], (128, 128)).T
    for s in range(8):
        lanes = pl.ds(s * 128, 128)
        x = pair[:, s].reshape(128, 128).astype(F32).T
        centred = x - jnp.mean(x, axis=0, keepdims=True)
        rstd = lax.rsqrt(jnp.mean(centred * centred, axis=0, keepdims=True) + EPS)
        hat = centred * rstd
        hat_in[:, lanes] = hat
        rstd_in[:, lanes] = rstd
        n = (hat * g_in[...]).astype(BF16)
        normed[:, lanes] = n
        p = dot(w_t[pl.ds(0, 512)], n)
        s0, p1 = jax.nn.sigmoid(p[0:128]), p[128:256]
        s2_, p3 = jax.nn.sigmoid(p[256:384]), p[384:512]
        gates[0, :, lanes] = s0
        gates[1, :, lanes] = p1
        gates[2, :, lanes] = s2_
        gates[3, :, lanes] = p3
        wide[:, s, :] = s0 * p1
        wide[:, 8 + s, :] = s2_ * p3
    sb1[...] = wide[...].astype(BF16)

    pl.semaphore_wait(barrier, 128)
    exchange(
        lambda r, c: sb1.at[r * 16 + c], rb1.at[rx, col // 4, col % 4], 0,
        sb1.at[me], rb1.at[rx, col // 4, col % 4],
    )

    ow_t[...] = out_weight[...].astype(F32).T.astype(BF16)
    g_out[...] = jnp.broadcast_to(gain_out[...], (128, 128)).T
    for s in range(8):
        lanes = pl.ds(s * 128, 128)
        gate = jax.nn.sigmoid(dot(w_t[pl.ds(512, 128)], normed[:, lanes]))
        gates[4, :, lanes] = gate
        cotangent = out_grad[:, s].reshape(128, 128).astype(F32).T
        og_t[:, lanes] = cotangent
        gpo = (cotangent * gate).astype(BF16)
        grad_po[:, lanes] = gpo
        grad_no[:, lanes] = dot(out_weight[...], gpo)

    arrive(sb1, recv.at[0])
    for g in range(4):
        tiles = [rb1[:, g, q].astype(F32) for q in range(4)]
        for a, tile in enumerate(swap_blocks(tiles)):
            left32[:, a, :, pl.ds(g * 128, 128)] = tile[:, 0:8]
            right32[:, a, :, pl.ds(g * 128, 128)] = tile[:, 8:16]
    edges[0, 0] = left32[...].reshape(256, 512).astype(BF16)
    edges[0, 1] = right32[...].reshape(256, 512).astype(BF16)
    copy_edges = to_sibling(edges.at[0], edges.at[1], 0)
    copy_edges.start()

    def send_mixed(slot):
        mixed = dot(edges[0, 0], edges[slot, 1], NT).reshape(8, 4, 8, 256)
        for g in range(2):
            tiles = swap_blocks([mixed[:, a, :, g * 128 : g * 128 + 128] for a in range(4)])
            for q in range(4):
                sb2[slot, :, g, q] = tiles[q].astype(BF16)

    send_mixed(0)
    copy_edges.wait()
    send_mixed(1)

    def mixed_tile(r, c):
        return sb2.at[(c % 2 + core) % 2, r, c // 8, (c // 2) % 4]

    exchange(mixed_tile, rb2.at[me], 1, mixed_tile(rx, col), rb2.at[me])
    arrive(rb2, recv.at[1])

    wide[:, 0:8, :] = rb2[...].astype(F32)
    gain_sum = jnp.zeros((128, 128), F32)
    for s in range(8):
        lanes = pl.ds(s * 128, 128)
        x = wide[:, s, :]
        centred = x - jnp.mean(x, axis=0, keepdims=True)
        rstd = lax.rsqrt(jnp.mean(centred * centred, axis=0, keepdims=True) + EPS)
        hat = centred * rstd
        gno = grad_no[:, lanes]
        gain_sum = gain_sum + gno * hat
        cot = gno * g_out[...]
        inner = jnp.mean(cot * hat, axis=0, keepdims=True)
        grad = rstd * (cot - jnp.mean(cot, axis=0, keepdims=True) - hat * inner)
        grad_no[:, lanes] = hat
        wide[:, 8 + s, :] = grad
    sb3[...] = wide[:, 8:16, :].astype(BF16)
    here = rb3.at[(col % 2 + core) % 2, rx, col // 8, (col // 2) % 4]
    exchange(lambda r, c: sb3.at[r * 16 + c], here, 2, sb3.at[me], here)
    gain_out_part = jnp.sum(gain_sum.T, axis=0, keepdims=True)

    for s in range(8):
        lanes = pl.ds(s * 128, 128)
        no = (grad_no[:, lanes] * g_out[...]).astype(BF16)
        sb_no = no
        grad_p[pl.ds(0, 128), lanes] = sb_no
        po = dot(ow_t[...], no)
        gate = gates[4, :, lanes]
        update_o[:, s] = (gate * po).T.reshape(4, 32, 128).astype(BF16)
        grad_p[pl.ds(512, 128), lanes] = (og_t[:, lanes] * po * (gate * (1.0 - gate))).astype(BF16)
    out_part = dot(grad_p[pl.ds(0, 128)], grad_po[...], NT)

    arrive(sb3, recv.at[2])
    for slot in range(2):
        for g in range(2):
            tiles = swap_blocks([rb3[slot, :, g, q].astype(F32) for q in range(4)])
            for a in range(4):
                left32[:, a, :, pl.ds(slot * 256 + g * 128, 128)] = tiles[a]
    for slot in range(2):
        grad_mat[slot] = left32[:, :, :, pl.ds(slot * 256, 256)].reshape(256, 256).astype(BF16)
    copy_grad = to_sibling(grad_mat.at[1], grad_far, 1)
    copy_grad.start()
    grad_left = dot(grad_mat[0], edges[0, 1]) + dot(grad_mat[1], edges[1, 1])
    left32[...] = grad_left.reshape(8, 4, 8, 512)
    grad_right = dot(grad_mat[0], edges[0, 0], TN)
    copy_grad.wait()
    grad_right = grad_right + dot(grad_far[...], edges[1, 0], TN)
    right32[...] = grad_right.reshape(8, 4, 8, 512)
    for g in range(4):
        lanes = pl.ds(g * 128, 128)
        tiles = swap_blocks(
            [jnp.concatenate([left32[:, a, :, lanes], right32[:, a, :, lanes]], axis=1) for a in range(4)]
        )
        for q in range(4):
            sb4[:, g, q] = tiles[q].astype(BF16)
    exchange(lambda r, c: sb4.at[r, c // 4, c % 4], rb4.at[me], 3, sb4.at[rx, col // 4, col % 4], rb4.at[me])

    gate_part = dot(normed[...], grad_p[pl.ds(512, 128)], NT)
    arrive(rb4, recv.at[3])
    wide[...] = rb4[...].astype(F32)
    gain_sum = jnp.zeros((128, 128), F32)
    for s in range(8):
        lanes = pl.ds(s * 128, 128)
        gl, gr = wide[:, s, :], wide[:, 8 + s, :]
        s0, p1 = gates[0, :, lanes], gates[1, :, lanes]
        s2_, p3 = gates[2, :, lanes], gates[3, :, lanes]
        dl, dr = gl * s0, gr * s2_
        grad_p[pl.ds(0, 128), lanes] = (dl * p1 * (1.0 - s0)).astype(BF16)
        grad_p[pl.ds(128, 128), lanes] = dl.astype(BF16)
        grad_p[pl.ds(256, 128), lanes] = (dr * p3 * (1.0 - s2_)).astype(BF16)
        grad_p[pl.ds(384, 128), lanes] = dr.astype(BF16)
        gni = dot(weight[...], grad_p[:, lanes])
        gain_sum = gain_sum + gni * hat_in[:, lanes]
        og_t[:, lanes] = gni
    gain_in_part = jnp.sum(gain_sum.T, axis=0, keepdims=True)
    in_part = dot(normed[...], grad_p[pl.ds(0, 512)], NT)
    blocks = [in_part[:, 0:128], in_part[:, 128:256], in_part[:, 256:384]]
    part[0, :, 0:24, :] = jnp.concatenate(blocks, axis=0).reshape(16, 24, 128)
    blocks = [in_part[:, 384:512], gate_part, out_part]
    part[1, :, 0:24, :] = jnp.concatenate(blocks, axis=0).reshape(16, 24, 128)
    index = lax.broadcasted_iota(jnp.int32, (8, 128), 0)
    gain_tile = jnp.where(index == 0, gain_in_part, jnp.where(index == 1, gain_out_part, 0.0))
    part[:, :, 24:32, :] = jnp.broadcast_to(gain_tile[None, None], (2, 16, 8, 128))

    copy_part = to_sibling(part.at[1 - core], part_far, 2)
    copy_part.start()
    for s in range(8):
        lanes = pl.ds(s * 128, 128)
        hat = hat_in[:, lanes]
        cot = og_t[:, lanes] * g_in[...]
        inner = jnp.mean(cot * hat, axis=0, keepdims=True)
        grad = rstd_in[:, lanes] * (cot - jnp.mean(cot, axis=0, keepdims=True) - hat * inner)
        pair_grad_o[:, s] = grad.T.reshape(4, 32, 128)
    copy_part.wait()
    s1[...] = (part[core] + part_far[...]).astype(BF16)

    def along_col(source, target, slot):
        def one(t, carry):
            c = (col + t) % 16
            pltpu.make_async_remote_copy(
                src_ref=source(c), dst_ref=target, send_sem=red_send.at[slot], recv_sem=red_recv.at[slot],
                device_id=(row, c), device_id_type=MESH,
            ).start()
            return carry

        lax.fori_loop(1, 16, one, 0)

    def all_of(view, semaphore):
        pltpu.make_async_copy(view, view, semaphore).wait()

    along_col(lambda c: s1.at[c], r1.at[col], 0)
    r1[col] = s1[col]
    all_of(r1.at[pl.ds(0, 15)], red_recv.at[0])
    s2[...] = jnp.sum(r1[...].astype(F32), axis=0).astype(BF16)

    def along_row(t, carry):
        r = (rx + t) % 8
        pltpu.make_async_remote_copy(
            src_ref=s2, dst_ref=r2.at[rx], send_sem=red_send.at[1], recv_sem=red_recv.at[1],
            device_id=(r * 2 + core, col), device_id_type=MESH,
        ).start()
        return carry

    lax.fori_loop(1, 8, along_row, 0)
    r2[rx] = s2[...]
    all_of(r2.at[pl.ds(0, 7)], red_recv.at[1])
    total = jnp.sum(r2[...].astype(F32), axis=0)
    gain_grad_o[...] = total[24:26]
    final[core, col] = total[0:24]
    along_col(lambda c: final.at[core, col], final.at[core, col], 2)
    all_of(final.at[core, pl.ds(0, 15)], red_recv.at[2])
    copy_final = to_sibling(final.at[core], final.at[core], 3)
    copy_final.start()
    copy_final.wait()
    first = final[0].reshape(384, 128)
    second = final[1].reshape(384, 128)
    for b in range(3):
        weight_grad_o[:, pl.ds(b * 128, 128)] = first[b * 128 : b * 128 + 128]
    for b in range(2):
        weight_grad_o[:, pl.ds(384 + b * 128, 128)] = second[b * 128 : b * 128 + 128]
    out_weight_grad_o[...] = second[256:384]

    arrive(sb1, send.at[0])
    arrive(rb2, send.at[1])
    arrive(sb3, send.at[2])
    arrive(rb4, send.at[3])
    all_of(r1.at[pl.ds(0, 15)], red_send.at[0])
    all_of(r2.at[pl.ds(0, 7)], red_send.at[1])
    all_of(final.at[core, pl.ds(0, 15)], red_send.at[2])


def on_device(pair, gain_in, in_weight, gain_out, out_weight, out_grad):
    vmem = pl.BlockSpec(memory_space=pltpu.VMEM)
    scratch = [
        ((128, 16, 128), F32),
        ((128, 16, 128), BF16),
        ((8, 4, 4, 16, 128), BF16),
        ((8, 4, 8, 512), F32),
        ((8, 4, 8, 512), F32),
        ((2, 2, 256, 512), BF16),
        ((2, 8, 2, 4, 8, 128), BF16),
        ((128, 8, 128), BF16),
        ((128, 8, 128), BF16),
        ((2, 8, 2, 4, 8, 128), BF16),
        ((2, 256, 256), BF16),
        ((256, 256), BF16),
        ((8, 4, 4, 16, 128), BF16),
        ((128, 16, 128), BF16),
        ((128, 1024), BF16),
        ((128, 1024), F32),
        ((1, 1024), F32),
        ((5, 128, 1024), F32),
        ((128, 1024), BF16),
        ((128, 1024), F32),
        ((128, 1024), F32),
        ((640, 1024), BF16),
        ((640, 128), BF16),
        ((128, 128), BF16),
        ((128, 128), F32),
        ((128, 128), F32),
        ((2, 16, 32, 128), F32),
        ((16, 32, 128), F32),
        ((16, 32, 128), BF16),
        ((16, 32, 128), BF16),
        ((32, 128), BF16),
        ((8, 32, 128), BF16),
        ((2, 16, 24, 128), F32),
    ]
    update, pair_grad, in_weight_grad, out_weight_grad, gain_grad = pl.pallas_call(
        kernel,
        out_shape=(
            jax.ShapeDtypeStruct((4, 8, 32, 128), BF16),
            jax.ShapeDtypeStruct((4, 8, 32, 128), F32),
            jax.ShapeDtypeStruct((128, 640), F32),
            jax.ShapeDtypeStruct((128, 128), F32),
            jax.ShapeDtypeStruct((2, 128), F32),
        ),
        in_specs=[vmem] * 6,
        out_specs=[vmem] * 5,
        scratch_shapes=[pltpu.VMEM(shape, kind) for shape, kind in scratch]
        + [pltpu.SemaphoreType.DMA((4,))] * 4
        + [pltpu.SemaphoreType.DMA((3,))] * 2,
        compiler_params=pltpu.CompilerParams(
            collective_id=0, has_side_effects=True, vmem_limit_bytes=48 * 2**20
        ),
    )(
        pair.reshape(4, 8, 32, 128), gain_in.reshape(1, 128), in_weight,
        gain_out.reshape(1, 128), out_weight, out_grad.reshape(4, 8, 32, 128),
    )
    return (
        update.reshape(32, 32, 128), pair_grad.reshape(32, 32, 128),
        in_weight_grad, out_weight_grad, gain_grad,
    )


def solution(mesh):
    return jax.shard_map(
        on_device,
        mesh=mesh,
        in_specs=(P("row", "col", None), P(), P(), P(), P(), P("row", "col", None)),
        out_specs=(P("row", "col", None), P("row", "col", None), P(), P(), P()),
        check_vma=False,
    )
```

```python
import jax
import jax.numpy as jnp
from jax import lax
from jax.experimental import pallas as pl
from jax.experimental.pallas import tpu as pltpu
from jax.sharding import PartitionSpec as P

EPS = 1e-05
MESH = pl.DeviceIdType.MESH
F32 = jnp.float32
BF16 = jnp.bfloat16
NT = (((1,), (1,)), ((), ()))
TN = (((0,), (0,)), ((), ()))


def dot(a, b, dims=(((1,), (0,)), ((), ()))):
    return lax.dot_general(a, b, dims, preferred_element_type=F32)


def swap_blocks(tiles):
    shape = tiles[0].shape
    flat = [t.reshape(-1, 128) for t in tiles]
    lane = lax.broadcasted_iota(jnp.int32, flat[0].shape, 1)
    low = lane < 64
    even = (lane // 32) % 2 == 0
    half = [None] * 4
    for q in range(2):
        a, b = flat[q], flat[q + 2]
        half[q] = jnp.where(low, a, pltpu.roll(b, 64, 1))
        half[q + 2] = jnp.where(low, pltpu.roll(a, 64, 1), b)
    out = [None] * 4
    for q in (0, 2):
        a, b = half[q], half[q + 1]
        out[q] = jnp.where(even, a, pltpu.roll(b, 32, 1))
        out[q + 1] = jnp.where(even, pltpu.roll(a, 96, 1), b)
    return [t.reshape(shape) for t in out]


def kernel(
    pair_h, gain_in_h, weight_h, gain_out_h, out_weight_h, out_grad_h,
    update_o, pair_grad_o, weight_grad_o, out_weight_grad_o, gain_grad_o,
    pair, weight, out_weight, out_grad, gain_in, gain_out,
    wide, sb1, rb1, edges, sb2, rb2, sb3, rb3, grad_mat, grad_far, sb4, rb4,
    normed, hat_in, rstd_in, gates, grad_po, grad_no, og_t, grad_p, w_t, ow_t, g_in, g_out,
    sb5, rb5, sums, sums_far, total_bf, final,
    load, send, recv, sib_send, sib_recv,
):
    row, col = lax.axis_index("row"), lax.axis_index("col")
    core, rx = lax.rem(row, 2), lax.div(row, 2)
    me = rx * 16 + col
    sibling = (rx * 2 + 1 - core, col)
    barrier = pltpu.get_barrier_semaphore()

    def partners(act):
        def line(dr, first):
            r = lax.rem(rx + dr, 8)

            def one(dc, carry):
                act(dr, r, lax.rem(col + dc, 16))
                return carry

            lax.fori_loop(first, 16, one, 0, unroll=True)

        def rest(dr, carry):
            line(dr, 0)
            return carry

        line(0, 1)
        lax.fori_loop(1, 8, rest, 0)

    def greet(dr, r, c):
        pl.semaphore_signal(barrier, inc=1, device_id=(r * 2 + core, c), device_id_type=MESH)

    loads = [
        pltpu.make_async_copy(source, target, load.at[i])
        for i, (source, target) in enumerate(
            [
                (pair_h, pair), (weight_h, weight), (out_weight_h, out_weight), (out_grad_h, out_grad),
                (gain_in_h, gain_in), (gain_out_h, gain_out),
            ]
        )
    ]
    for copy in loads:
        copy.start()
    partners(greet)
    pl.semaphore_signal(barrier, inc=1, device_id=sibling, device_id_type=MESH)

    def exchange(source, target, slot):
        def one(dr, r, c):
            pltpu.make_async_remote_copy(
                src_ref=source.at[r * 16 + c], dst_ref=target.at[me], send_sem=send.at[slot],
                recv_sem=recv.at[slot, dr], device_id=(r * 2 + core, c), device_id_type=MESH,
            ).start()

        partners(one)
        target[me] = source[me]

    def drain(buffer, count, semaphore):
        view = buffer.at[pl.ds(0, count)]
        pltpu.make_async_copy(view, view, semaphore).wait()

    def arrive(buffer, slot):
        drain(buffer, 15, recv.at[slot, 0])

        def one(dr, carry):
            drain(buffer, 16, recv.at[slot, dr])
            return carry

        lax.fori_loop(1, 8, one, 0)

    def to_sibling(source, target, slot):
        return pltpu.make_async_remote_copy(
            src_ref=source, dst_ref=target, send_sem=sib_send.at[slot], recv_sem=sib_recv.at[slot],
            device_id=sibling, device_id_type=MESH,
        )

    loads[4].wait()
    loads[5].wait()
    g_in[...] = jnp.broadcast_to(gain_in[...], (128, 128)).T
    g_out[...] = jnp.broadcast_to(gain_out[...], (128, 128)).T
    loads[0].wait()
    loads[1].wait()
    w_t[...] = weight[...].astype(F32).T.astype(BF16)
    for s in range(8):
        lanes = pl.ds(s * 128, 128)
        x = pair[:, s].reshape(128, 128).astype(F32).T
        centred = x - jnp.mean(x, axis=0, keepdims=True)
        rstd = lax.rsqrt(jnp.mean(centred * centred, axis=0, keepdims=True) + EPS)
        hat = centred * rstd
        hat_in[:, lanes] = hat
        rstd_in[:, lanes] = rstd
        n = (hat * g_in[...]).astype(BF16)
        normed[:, lanes] = n
        p = dot(w_t[pl.ds(0, 512)], n)
        s0, p1 = jax.nn.sigmoid(p[0:128]), p[128:256]
        s2, p3 = jax.nn.sigmoid(p[256:384]), p[384:512]
        gates[0, :, lanes] = s0
        gates[1, :, lanes] = p1
        gates[2, :, lanes] = s2
        gates[3, :, lanes] = p3
        wide[:, s, :] = s0 * p1
        wide[:, 8 + s, :] = s2 * p3
    sb1[...] = wide[...].astype(BF16)

    pl.semaphore_wait(barrier, 128)
    exchange(sb1, rb1, 0)

    loads[2].wait()
    loads[3].wait()
    ow_t[...] = out_weight[...].astype(F32).T.astype(BF16)
    for s in range(8):
        lanes = pl.ds(s * 128, 128)
        gate = jax.nn.sigmoid(dot(w_t[pl.ds(512, 128)], normed[:, lanes]))
        gates[4, :, lanes] = gate
        cotangent = out_grad[:, s].reshape(128, 128).astype(F32).T
        og_t[:, lanes] = cotangent
        gpo = (cotangent * gate).astype(BF16)
        grad_po[:, lanes] = gpo
        grad_no[:, lanes] = dot(out_weight[...], gpo)

    def edge_rows(dr):
        r = lax.rem(rx + 8 - dr, 8)
        parts = []
        for g in range(4):
            parts.append(swap_blocks([rb1[r * 16 + 4 * g + q].astype(F32) for q in range(4)]))
        for side in range(2):
            rows = [
                jnp.concatenate([parts[g][a][8 * side : 8 * side + 8] for g in range(4)], axis=1)
                for a in range(4)
            ]
            edges[0, side, r] = jnp.concatenate(rows, axis=0).astype(BF16)
            to_sibling(edges.at[0, side, r], edges.at[1, side, r], side).start()

    drain(sb1, 15, recv.at[0, 0])
    edge_rows(0)

    def edge_group(dr, carry):
        drain(sb1, 16, recv.at[0, dr])
        edge_rows(dr)
        return carry

    lax.fori_loop(1, 8, edge_group, 0)

    def side_of(slot, side):
        return edges[slot, side].reshape(256, 512)

    def place(slot):
        return core if slot == 0 else 1 - core

    def send_mixed(slot):
        mixed = dot(side_of(0, 0), side_of(slot, 1), NT).reshape(8, 4, 8, 256)
        for g in range(2):
            tiles = swap_blocks([mixed[:, a, :, g * 128 : g * 128 + 128] for a in range(4)])
            for q in range(4):
                sb2.reshape(8, 16, 8, 128)[:, 2 * (4 * g + q) + place(slot)] = tiles[q].astype(BF16)

    send_mixed(0)
    to_sibling(edges.at[0, 1], edges.at[1, 1], 1).wait_recv()
    send_mixed(1)
    exchange(sb2, rb2, 1)
    arrive(rb2, 1)

    wide[:, 0:8, :] = rb2[...].astype(F32)
    gain_sum = jnp.zeros((128, 128), F32)
    for s in range(8):
        lanes = pl.ds(s * 128, 128)
        x = wide[:, s, :]
        centred = x - jnp.mean(x, axis=0, keepdims=True)
        rstd = lax.rsqrt(jnp.mean(centred * centred, axis=0, keepdims=True) + EPS)
        hat = centred * rstd
        gno = grad_no[:, lanes]
        gain_sum = gain_sum + gno * hat
        cot = gno * g_out[...]
        inner = jnp.mean(cot * hat, axis=0, keepdims=True)
        grad = rstd * (cot - jnp.mean(cot, axis=0, keepdims=True) - hat * inner)
        grad_no[:, lanes] = hat
        wide[:, 8 + s, :] = grad
    sb3[...] = wide[:, 8:16, :].astype(BF16)
    exchange(sb3, rb3, 2)

    gain_out_part = jnp.sum(gain_sum.T, axis=0, keepdims=True)
    for s in range(8):
        lanes = pl.ds(s * 128, 128)
        no = (grad_no[:, lanes] * g_out[...]).astype(BF16)
        grad_p[pl.ds(0, 128), lanes] = no
        po = dot(ow_t[...], no)
        gate = gates[4, :, lanes]
        update_o[:, s] = (gate * po).T.reshape(4, 32, 128).astype(BF16)
        grad_p[pl.ds(512, 128), lanes] = (og_t[:, lanes] * po * (gate * (1.0 - gate))).astype(BF16)

    def grad_rows(dr):
        r = lax.rem(rx + 8 - dr, 8)
        for slot in range(2):
            parts = []
            for g in range(2):
                parts.append(
                    swap_blocks([rb3[r * 16 + 2 * (4 * g + q) + place(slot)].astype(F32) for q in range(4)])
                )
            rows = [jnp.concatenate([parts[0][a], parts[1][a]], axis=1) for a in range(4)]
            grad_mat[slot, r] = jnp.concatenate(rows, axis=0).astype(BF16)
        to_sibling(grad_mat.at[1, r], grad_far.at[r], 2).start()

    drain(sb3, 15, recv.at[2, 0])
    grad_rows(0)

    def grad_group(dr, carry):
        drain(sb3, 16, recv.at[2, dr])
        grad_rows(dr)
        return carry

    lax.fori_loop(1, 8, grad_group, 0)
    to_sibling(edges.at[0, 0], edges.at[1, 0], 0).wait_recv()
    near, other = grad_mat[0].reshape(256, 256), grad_mat[1].reshape(256, 256)
    grad_left = (dot(near, side_of(0, 1)) + dot(other, side_of(1, 1))).reshape(8, 4, 8, 512)
    grad_right = dot(near, side_of(0, 0), TN)
    to_sibling(grad_mat.at[1], grad_far, 2).wait_recv()
    grad_right = (grad_right + dot(grad_far[...].reshape(256, 256), side_of(1, 0), TN)).reshape(8, 4, 8, 512)
    for g in range(4):
        lanes = slice(g * 128, g * 128 + 128)
        tiles = swap_blocks(
            [jnp.concatenate([grad_left[:, a, :, lanes], grad_right[:, a, :, lanes]], axis=1) for a in range(4)]
        )
        for q in range(4):
            sb4.reshape(8, 16, 16, 128)[:, 4 * g + q] = tiles[q].astype(BF16)
    exchange(sb4, rb4, 3)

    out_part = dot(grad_p[pl.ds(0, 128)], grad_po[...], NT)
    gate_part = dot(normed[...], grad_p[pl.ds(512, 128)], NT)
    sums[:, 4, :] = gate_part
    sums[:, 5, :] = out_part
    sums[:, 7, :] = jnp.broadcast_to(gain_out_part, (128, 128))

    arrive(rb4, 3)
    wide[...] = rb4[...].astype(F32)
    gain_sum = jnp.zeros((128, 128), F32)
    for s in range(8):
        lanes = pl.ds(s * 128, 128)
        gl, gr = wide[:, s, :], wide[:, 8 + s, :]
        s0, p1 = gates[0, :, lanes], gates[1, :, lanes]
        s2, p3 = gates[2, :, lanes], gates[3, :, lanes]
        dl, dr = gl * s0, gr * s2
        grad_p[pl.ds(0, 128), lanes] = (dl * p1 * (1.0 - s0)).astype(BF16)
        grad_p[pl.ds(128, 128), lanes] = dl.astype(BF16)
        grad_p[pl.ds(256, 128), lanes] = (dr * p3 * (1.0 - s2)).astype(BF16)
        grad_p[pl.ds(384, 128), lanes] = dr.astype(BF16)
        gni = dot(weight[...], grad_p[:, lanes])
        gain_sum = gain_sum + gni * hat_in[:, lanes]
        og_t[:, lanes] = gni
    gain_in_part = jnp.sum(gain_sum.T, axis=0, keepdims=True)
    in_part = dot(normed[...], grad_p[pl.ds(0, 512)], NT)
    for b in range(4):
        sums[:, b, :] = in_part[:, b * 128 : b * 128 + 128]
    sums[:, 6, :] = jnp.broadcast_to(gain_in_part, (128, 128))

    sb5[...] = sums[...].astype(BF16)
    exchange(sb5, rb5, 4)
    for s in range(8):
        lanes = pl.ds(s * 128, 128)
        hat = hat_in[:, lanes]
        cot = og_t[:, lanes] * g_in[...]
        inner = jnp.mean(cot * hat, axis=0, keepdims=True)
        grad = rstd_in[:, lanes] * (cot - jnp.mean(cot, axis=0, keepdims=True) - hat * inner)
        pair_grad_o[:, s] = grad.T.reshape(4, 32, 128)
    arrive(rb5, 4)
    sums[0] = jnp.sum(rb5[...].astype(F32), axis=0)
    copy_sums = to_sibling(sums.at[0], sums_far, 3)
    copy_sums.start()
    copy_sums.wait()
    total = sums[0] + sums_far[...]
    gain_grad_o[...] = total[6:8]
    total_bf[...] = total.astype(BF16)
    final[me] = total_bf[...]

    def gather(dr, r, c):
        pltpu.make_async_remote_copy(
            src_ref=total_bf, dst_ref=final.at[me], send_sem=send.at[5], recv_sem=recv.at[5, dr],
            device_id=(r * 2 + core, c), device_id_type=MESH,
        ).start()

    partners(gather)
    drain(sb1, 127, send.at[0])
    drain(rb2, 127, send.at[1])
    drain(sb3, 127, send.at[2])
    drain(rb4, 127, send.at[3])
    drain(sb5, 127, send.at[4])
    for side in range(2):
        to_sibling(edges.at[0, side], edges.at[1, side], side).wait_send()
    to_sibling(grad_mat.at[1], grad_far, 2).wait_send()
    arrive(rb5, 5)
    sums[...] = final[...].astype(F32)
    for b in range(5):
        weight_grad_o[:, pl.ds(b * 128, 128)] = sums[:, b, :]
    out_weight_grad_o[...] = sums[:, 5, :]
    drain(rb5, 127, send.at[5])


def write_out(*refs):
    count = len(refs) // 2
    copies = [
        pltpu.make_async_copy(refs[i], refs[count + i], refs[-1].at[i]) for i in range(count)
    ]
    for copy in copies:
        copy.start()
    for copy in copies:
        copy.wait()


def on_device(pair, gain_in, in_weight, gain_out, out_weight, out_grad):
    vmem = pl.BlockSpec(memory_space=pltpu.VMEM)
    hbm = pl.BlockSpec(memory_space=pltpu.HBM)
    scratch = [
        ((4, 8, 32, 128), BF16),
        ((128, 640), BF16),
        ((128, 128), BF16),
        ((4, 8, 32, 128), BF16),
        ((1, 128), F32),
        ((1, 128), F32),
        ((128, 16, 128), F32),
        ((128, 16, 128), BF16),
        ((128, 16, 128), BF16),
        ((2, 2, 8, 32, 512), BF16),
        ((128, 8, 128), BF16),
        ((128, 8, 128), BF16),
        ((128, 8, 128), BF16),
        ((128, 8, 128), BF16),
        ((2, 8, 32, 256), BF16),
        ((8, 32, 256), BF16),
        ((128, 16, 128), BF16),
        ((128, 16, 128), BF16),
        ((128, 1024), BF16),
        ((128, 1024), F32),
        ((1, 1024), F32),
        ((5, 128, 1024), F32),
        ((128, 1024), BF16),
        ((128, 1024), F32),
        ((128, 1024), F32),
        ((640, 1024), BF16),
        ((640, 128), BF16),
        ((128, 128), BF16),
        ((128, 128), F32),
        ((128, 128), F32),
        ((128, 8, 128), BF16),
        ((128, 8, 128), BF16),
        ((128, 8, 128), F32),
        ((8, 128), F32),
        ((8, 128), BF16),
        ((128, 8, 128), BF16),
    ]
    shapes = (
        jax.ShapeDtypeStruct((4, 8, 32, 128), BF16),
        jax.ShapeDtypeStruct((4, 8, 32, 128), F32),
        jax.ShapeDtypeStruct((128, 640), F32),
        jax.ShapeDtypeStruct((128, 128), F32),
        jax.ShapeDtypeStruct((2, 128), F32),
    )
    operands = [
        pltpu.with_memory_space_constraint(value, pltpu.HBM)
        for value in (
            pair.reshape(4, 8, 32, 128), gain_in.reshape(1, 128), in_weight,
            gain_out.reshape(1, 128), out_weight, out_grad.reshape(4, 8, 32, 128),
        )
    ]
    results = pl.pallas_call(
        kernel,
        out_shape=shapes,
        in_specs=[hbm] * 6,
        out_specs=[vmem] * 5,
        scratch_shapes=[pltpu.VMEM(shape, kind) for shape, kind in scratch]
        + [
            pltpu.SemaphoreType.DMA((6,)),
            pltpu.SemaphoreType.DMA((6,)),
            pltpu.SemaphoreType.DMA((6, 8)),
            pltpu.SemaphoreType.DMA((4,)),
            pltpu.SemaphoreType.DMA((4,)),
        ],
        compiler_params=pltpu.CompilerParams(
            collective_id=0, has_side_effects=True, vmem_limit_bytes=48 * 2**20
        ),
    )(*operands)
    update, pair_grad, in_weight_grad, out_weight_grad, gain_grad = pl.pallas_call(
        write_out,
        out_shape=shapes,
        in_specs=[vmem] * 5,
        out_specs=[hbm] * 5,
        scratch_shapes=[pltpu.SemaphoreType.DMA((5,))],
        compiler_params=pltpu.CompilerParams(vmem_limit_bytes=16 * 2**20),
    )(*results)
    return (
        update.reshape(32, 32, 128), pair_grad.reshape(32, 32, 128),
        in_weight_grad, out_weight_grad, gain_grad,
    )


def solution(mesh):
    return jax.shard_map(
        on_device,
        mesh=mesh,
        in_specs=(P("row", "col", None), P(), P(), P(), P(), P("row", "col", None)),
        out_specs=(P("row", "col", None), P("row", "col", None), P(), P(), P()),
        check_vma=False,
    )
```

```python
import jax
import jax.numpy as jnp
from jax import lax
from jax.experimental import pallas as pl
from jax.experimental.pallas import tpu as pltpu
from jax.sharding import PartitionSpec as P

EPS = 1e-05
MESH = pl.DeviceIdType.MESH
F32 = jnp.float32
BF16 = jnp.bfloat16
NT = (((1,), (1,)), ((), ()))
TN = (((0,), (0,)), ((), ()))


def dot(a, b, dims=(((1,), (0,)), ((), ()))):
    return lax.dot_general(a, b, dims, preferred_element_type=F32)


def swap_blocks(tiles):
    shape = tiles[0].shape
    flat = [t.reshape(-1, 128) for t in tiles]
    lane = lax.broadcasted_iota(jnp.int32, flat[0].shape, 1)
    low = lane < 64
    even = (lane // 32) % 2 == 0
    half = [None] * 4
    for q in range(2):
        a, b = flat[q], flat[q + 2]
        half[q] = jnp.where(low, a, pltpu.roll(b, 64, 1))
        half[q + 2] = jnp.where(low, pltpu.roll(a, 64, 1), b)
    out = [None] * 4
    for q in (0, 2):
        a, b = half[q], half[q + 1]
        out[q] = jnp.where(even, a, pltpu.roll(b, 32, 1))
        out[q + 1] = jnp.where(even, pltpu.roll(a, 96, 1), b)
    return [t.reshape(shape) for t in out]


def kernel(
    pair_h, gain_in_h, weight_h, gain_out_h, out_weight_h, out_grad_h,
    update_o, pair_grad_o, weight_grad_o, out_weight_grad_o, gain_grad_o,
    pair, weight, out_weight, out_grad, gain_in, gain_out,
    wide, sb1, rb1, edges, sb2, rb2, sb3, rb3, grad_mat, grad_far, sb4, rb4,
    normed, hat_in, rstd_in, gates, grad_po, grad_no, og_t, grad_p, w_t, ow_t, g_in, g_out,
    sb5, rb5, sums, plane_sum, planes, total_bf, final,
    load, send, recv, sib_send, sib_recv,
):
    row, col = lax.axis_index("row"), lax.axis_index("col")
    core, rx = lax.rem(row, 2), lax.div(row, 2)
    me = rx * 16 + col
    half, z = lax.div(col, 2), lax.rem(col, 8)
    spot = lax.div(col, 8) * 16 + row
    sibling = (rx * 2 + 1 - core, col)
    barrier = pltpu.get_barrier_semaphore()

    def partners(act):
        def line(dr, first):
            r = lax.rem(rx + dr, 8)

            def one(dc, carry):
                act(dr, r, lax.rem(col + dc, 16))
                return carry

            lax.fori_loop(first, 16, one, 0, unroll=True)

        def rest(dr, carry):
            line(dr, 0)
            return carry

        line(0, 1)
        lax.fori_loop(1, 8, rest, 0)

    def greet(dr, r, c):
        pl.semaphore_signal(barrier, inc=1, device_id=(r * 2 + core, c), device_id_type=MESH)

    loads = [
        pltpu.make_async_copy(source, target, load.at[i])
        for i, (source, target) in enumerate(
            [
                (pair_h, pair), (weight_h, weight), (out_weight_h, out_weight), (out_grad_h, out_grad),
                (gain_in_h, gain_in), (gain_out_h, gain_out),
            ]
        )
    ]
    for copy in loads:
        copy.start()
    partners(greet)

    def in_plane(d):
        p = lax.rem(spot + d, 32)
        return p, (lax.rem(p, 16), lax.div(p, 16) * 8 + z)

    def greet_plane(d, carry):
        pl.semaphore_signal(barrier, inc=1, device_id=in_plane(2 * d + 1)[1], device_id_type=MESH)
        return carry

    lax.fori_loop(0, 16, greet_plane, 0, unroll=True)

    def exchange(source, target, slot):
        def one(dr, r, c):
            pltpu.make_async_remote_copy(
                src_ref=source.at[r * 16 + c], dst_ref=target.at[me], send_sem=send.at[slot],
                recv_sem=recv.at[slot, dr], device_id=(r * 2 + core, c), device_id_type=MESH,
            ).start()

        partners(one)
        target[me] = source[me]

    def drain(buffer, count, semaphore):
        view = buffer.at[pl.ds(0, count)]
        pltpu.make_async_copy(view, view, semaphore).wait()

    def arrive(buffer, slot):
        drain(buffer, 15, recv.at[slot, 0])

        def one(dr, carry):
            drain(buffer, 16, recv.at[slot, dr])
            return carry

        lax.fori_loop(1, 8, one, 0)

    def to_sibling(source, target, slot):
        return pltpu.make_async_remote_copy(
            src_ref=source, dst_ref=target, send_sem=sib_send.at[slot], recv_sem=sib_recv.at[slot],
            device_id=sibling, device_id_type=MESH,
        )

    loads[4].wait()
    loads[5].wait()
    g_in[...] = jnp.broadcast_to(gain_in[...], (128, 128)).T
    g_out[...] = jnp.broadcast_to(gain_out[...], (128, 128)).T
    loads[0].wait()
    loads[1].wait()
    w_t[...] = weight[...].astype(F32).T.astype(BF16)
    for s in range(8):
        lanes = pl.ds(s * 128, 128)
        x = pair[:, s].reshape(128, 128).astype(F32).T
        centred = x - jnp.mean(x, axis=0, keepdims=True)
        rstd = lax.rsqrt(jnp.mean(centred * centred, axis=0, keepdims=True) + EPS)
        hat = centred * rstd
        hat_in[:, lanes] = hat
        rstd_in[:, lanes] = rstd
        n = (hat * g_in[...]).astype(BF16)
        normed[:, lanes] = n
        p = dot(w_t[pl.ds(0, 512)], n)
        s0, p1 = jax.nn.sigmoid(p[0:128]), p[128:256]
        s2, p3 = jax.nn.sigmoid(p[256:384]), p[384:512]
        gates[0, :, lanes] = s0
        gates[1, :, lanes] = p1
        gates[2, :, lanes] = s2
        gates[3, :, lanes] = p3
        wide[:, s, :] = s0 * p1
        wide[:, 8 + s, :] = s2 * p3
    sb1[...] = wide[...].astype(BF16)

    pl.semaphore_wait(barrier, 143)
    exchange(sb1, rb1, 0)

    loads[2].wait()
    loads[3].wait()
    ow_t[...] = out_weight[...].astype(F32).T.astype(BF16)
    for s in range(8):
        lanes = pl.ds(s * 128, 128)
        gate = jax.nn.sigmoid(dot(w_t[pl.ds(512, 128)], normed[:, lanes]))
        gates[4, :, lanes] = gate
        cotangent = out_grad[:, s].reshape(128, 128).astype(F32).T
        og_t[:, lanes] = cotangent
        gpo = (cotangent * gate).astype(BF16)
        grad_po[:, lanes] = gpo
        grad_no[:, lanes] = dot(out_weight[...], gpo)

    def edge_rows(dr):
        r = lax.rem(rx + 8 - dr, 8)
        parts = []
        for g in range(4):
            parts.append(swap_blocks([rb1[r * 16 + 4 * g + q].astype(F32) for q in range(4)]))
        for side in range(2):
            rows = [
                jnp.concatenate([parts[g][a][8 * side : 8 * side + 8] for g in range(4)], axis=1)
                for a in range(4)
            ]
            edges[0, side, r] = jnp.concatenate(rows, axis=0).astype(BF16)
            to_sibling(edges.at[0, side, r], edges.at[1, side, r], side).start()

    drain(sb1, 15, recv.at[0, 0])
    edge_rows(0)

    def edge_group(dr, carry):
        drain(sb1, 16, recv.at[0, dr])
        edge_rows(dr)
        return carry

    lax.fori_loop(1, 8, edge_group, 0)

    def side_of(slot, side):
        return edges[slot, side].reshape(256, 512)

    def place(slot):
        return core if slot == 0 else 1 - core

    def send_mixed(slot):
        mixed = dot(side_of(0, 0), side_of(slot, 1), NT).reshape(8, 4, 8, 256)
        for g in range(2):
            tiles = swap_blocks([mixed[:, a, :, g * 128 : g * 128 + 128] for a in range(4)])
            for q in range(4):
                sb2.reshape(8, 16, 8, 128)[:, 2 * (4 * g + q) + place(slot)] = tiles[q].astype(BF16)

    def exchange_mixed(slot):
        parity = place(slot)

        def start(dr, r, c):
            pltpu.make_async_remote_copy(
                src_ref=sb2.at[r * 16 + c], dst_ref=rb2.at[me], send_sem=send.at[1], recv_sem=recv.at[1, dr],
                device_id=(r * 2 + core, c), device_id_type=MESH,
            ).start()

        def line(dr, first):
            r = lax.rem(rx + dr, 8)

            def one(k, carry):
                start(dr, r, 2 * lax.rem(half + k, 8) + parity)
                return carry

            lax.fori_loop(first, 8, one, 0, unroll=True)

        def rest(dr, carry):
            line(dr, 0)
            return carry

        line(0, 1)

        @pl.when(parity != lax.rem(col, 2))
        def _():
            start(0, rx, 2 * half + parity)

        lax.fori_loop(1, 8, rest, 0)

    send_mixed(0)
    exchange_mixed(0)
    to_sibling(edges.at[0, 1], edges.at[1, 1], 1).wait_recv()
    send_mixed(1)
    exchange_mixed(1)
    rb2[me] = sb2[me]
    arrive(rb2, 1)

    wide[:, 0:8, :] = rb2[...].astype(F32)
    gain_sum = jnp.zeros((128, 128), F32)
    for s in range(8):
        lanes = pl.ds(s * 128, 128)
        x = wide[:, s, :]
        centred = x - jnp.mean(x, axis=0, keepdims=True)
        rstd = lax.rsqrt(jnp.mean(centred * centred, axis=0, keepdims=True) + EPS)
        hat = centred * rstd
        gno = grad_no[:, lanes]
        gain_sum = gain_sum + gno * hat
        cot = gno * g_out[...]
        inner = jnp.mean(cot * hat, axis=0, keepdims=True)
        grad = rstd * (cot - jnp.mean(cot, axis=0, keepdims=True) - hat * inner)
        grad_no[:, lanes] = hat
        wide[:, 8 + s, :] = grad
    sb3[...] = wide[:, 8:16, :].astype(BF16)
    exchange(sb3, rb3, 2)

    gain_out_part = jnp.sum(gain_sum.T, axis=0, keepdims=True)
    for s in range(8):
        lanes = pl.ds(s * 128, 128)
        no = (grad_no[:, lanes] * g_out[...]).astype(BF16)
        grad_p[pl.ds(0, 128), lanes] = no
        po = dot(ow_t[...], no)
        gate = gates[4, :, lanes]
        update_o[:, s] = (gate * po).T.reshape(4, 32, 128).astype(BF16)
        grad_p[pl.ds(512, 128), lanes] = (og_t[:, lanes] * po * (gate * (1.0 - gate))).astype(BF16)

    def grad_rows(dr):
        r = lax.rem(rx + 8 - dr, 8)
        for slot in range(2):
            parts = []
            for g in range(2):
                parts.append(
                    swap_blocks([rb3[r * 16 + 2 * (4 * g + q) + place(slot)].astype(F32) for q in range(4)])
                )
            rows = [jnp.concatenate([parts[0][a], parts[1][a]], axis=1) for a in range(4)]
            grad_mat[slot, r] = jnp.concatenate(rows, axis=0).astype(BF16)
        to_sibling(grad_mat.at[1, r], grad_far.at[r], 2).start()

    drain(sb3, 15, recv.at[2, 0])
    grad_rows(0)

    def grad_group(dr, carry):
        drain(sb3, 16, recv.at[2, dr])
        grad_rows(dr)
        return carry

    lax.fori_loop(1, 8, grad_group, 0)
    to_sibling(edges.at[0, 0], edges.at[1, 0], 0).wait_recv()
    near, other = grad_mat[0].reshape(256, 256), grad_mat[1].reshape(256, 256)
    grad_left = (dot(near, side_of(0, 1)) + dot(other, side_of(1, 1))).reshape(8, 4, 8, 512)
    grad_right = dot(near, side_of(0, 0), TN)
    to_sibling(grad_mat.at[1], grad_far, 2).wait_recv()
    grad_right = (grad_right + dot(grad_far[...].reshape(256, 256), side_of(1, 0), TN)).reshape(8, 4, 8, 512)
    for g in range(4):
        lanes = slice(g * 128, g * 128 + 128)
        tiles = swap_blocks(
            [jnp.concatenate([grad_left[:, a, :, lanes], grad_right[:, a, :, lanes]], axis=1) for a in range(4)]
        )
        for q in range(4):
            sb4.reshape(8, 16, 16, 128)[:, 4 * g + q] = tiles[q].astype(BF16)
    exchange(sb4, rb4, 3)

    out_part = dot(grad_p[pl.ds(0, 128)], grad_po[...], NT)
    gate_part = dot(normed[...], grad_p[pl.ds(512, 128)], NT)
    sums[:, 4, :] = gate_part
    sums[:, 5, :] = out_part
    sums[:, 7, :] = jnp.broadcast_to(gain_out_part, (128, 128))

    def edge_grads(dr):
        first = pl.multiple_of(lax.rem(rx + 8 - dr, 8) * 16, 16)
        here = pl.ds(first, 16)
        wide[here] = rb4[here].astype(F32)
        for s in range(8):
            lanes = pl.ds(s * 128, 128)
            gl, gr = wide[here, s, :], wide[here, 8 + s, :]
            s0, p1 = gates[0, here, lanes], gates[1, here, lanes]
            s2, p3 = gates[2, here, lanes], gates[3, here, lanes]
            dl, dr_ = gl * s0, gr * s2
            grad_p[here, lanes] = (dl * p1 * (1.0 - s0)).astype(BF16)
            grad_p[pl.ds(128 + first, 16), lanes] = dl.astype(BF16)
            grad_p[pl.ds(256 + first, 16), lanes] = (dr_ * p3 * (1.0 - s2)).astype(BF16)
            grad_p[pl.ds(384 + first, 16), lanes] = dr_.astype(BF16)

    def edge_grad_group(dr, carry):
        drain(rb4, 16, recv.at[3, dr])
        edge_grads(dr)
        return carry

    drain(rb4, 15, recv.at[3, 0])
    edge_grads(0)
    lax.fori_loop(1, 8, edge_grad_group, 0)
    gain_sum = jnp.zeros((128, 128), F32)
    for s in range(8):
        lanes = pl.ds(s * 128, 128)
        gni = dot(weight[...], grad_p[:, lanes])
        gain_sum = gain_sum + gni * hat_in[:, lanes]
        og_t[:, lanes] = gni
    gain_in_part = jnp.sum(gain_sum.T, axis=0, keepdims=True)
    in_part = dot(normed[...], grad_p[pl.ds(0, 512)], NT)
    for b in range(4):
        sums[:, b, :] = in_part[:, b * 128 : b * 128 + 128]
    sums[:, 6, :] = jnp.broadcast_to(gain_in_part, (128, 128))

    def along_plane(source, target, slot):
        def one(d, carry):
            p, device = in_plane(d)
            pltpu.make_async_remote_copy(
                src_ref=source(p), dst_ref=target, send_sem=send.at[slot], recv_sem=recv.at[slot, 0],
                device_id=device, device_id_type=MESH,
            ).start()
            return carry

        lax.fori_loop(1, 32, one, 0, unroll=True)

    def rows_of(p):
        return pl.ds(pl.multiple_of(p * 4, 4), 4)

    sb5[...] = sums[...].astype(BF16)
    along_plane(lambda p: sb5.at[rows_of(p)], rb5.at[spot], 4)
    rb5[spot] = sb5[rows_of(spot)]
    for s in range(8):
        lanes = pl.ds(s * 128, 128)
        hat = hat_in[:, lanes]
        cot = og_t[:, lanes] * g_in[...]
        inner = jnp.mean(cot * hat, axis=0, keepdims=True)
        grad = rstd_in[:, lanes] * (cot - jnp.mean(cot, axis=0, keepdims=True) - hat * inner)
        pair_grad_o[:, s] = grad.T.reshape(4, 32, 128)
    drain(rb5, 31, recv.at[4, 0])
    plane_sum[...] = jnp.sum(rb5[...].astype(F32), axis=0).astype(BF16)

    def along_z(d, carry):
        pltpu.make_async_remote_copy(
            src_ref=plane_sum, dst_ref=planes.at[z], send_sem=send.at[5], recv_sem=recv.at[5, 0],
            device_id=(row, lax.div(col, 8) * 8 + lax.rem(z + d, 8)), device_id_type=MESH,
        ).start()
        return carry

    lax.fori_loop(1, 8, along_z, 0, unroll=True)
    planes[z] = plane_sum[...]
    drain(planes, 7, recv.at[5, 0])
    total = jnp.sum(planes[...].astype(F32), axis=0)
    gain_grad_o[...] = total[0, 6:8]
    total_bf[...] = total.astype(BF16)
    along_plane(lambda p: total_bf, final.at[rows_of(spot)], 6)
    final[rows_of(spot)] = total_bf[...]
    drain(sb1, 127, send.at[0])
    drain(rb2, 127, send.at[1])
    drain(sb3, 127, send.at[2])
    drain(rb4, 127, send.at[3])
    drain(rb5, 31, send.at[4])
    drain(planes, 7, send.at[5])
    drain(rb5, 31, send.at[6])
    for side in range(2):
        to_sibling(edges.at[0, side], edges.at[1, side], side).wait_send()
    to_sibling(grad_mat.at[1], grad_far, 2).wait_send()
    drain(rb5, 31, recv.at[6, 0])
    sums[...] = final[...].astype(F32)
    for b in range(5):
        weight_grad_o[:, pl.ds(b * 128, 128)] = sums[:, b, :]
    out_weight_grad_o[...] = sums[:, 5, :]


def write_out(*refs):
    count = len(refs) // 2
    copies = [
        pltpu.make_async_copy(refs[i], refs[count + i], refs[-1].at[i]) for i in range(count)
    ]
    for copy in copies:
        copy.start()
    for copy in copies:
        copy.wait()


def on_device(pair, gain_in, in_weight, gain_out, out_weight, out_grad):
    vmem = pl.BlockSpec(memory_space=pltpu.VMEM)
    hbm = pl.BlockSpec(memory_space=pltpu.HBM)
    scratch = [
        ((4, 8, 32, 128), BF16),
        ((128, 640), BF16),
        ((128, 128), BF16),
        ((4, 8, 32, 128), BF16),
        ((1, 128), F32),
        ((1, 128), F32),
        ((128, 16, 128), F32),
        ((128, 16, 128), BF16),
        ((128, 16, 128), BF16),
        ((2, 2, 8, 32, 512), BF16),
        ((128, 8, 128), BF16),
        ((128, 8, 128), BF16),
        ((128, 8, 128), BF16),
        ((128, 8, 128), BF16),
        ((2, 8, 32, 256), BF16),
        ((8, 32, 256), BF16),
        ((128, 16, 128), BF16),
        ((128, 16, 128), BF16),
        ((128, 1024), BF16),
        ((128, 1024), F32),
        ((1, 1024), F32),
        ((5, 128, 1024), F32),
        ((128, 1024), BF16),
        ((128, 1024), F32),
        ((128, 1024), F32),
        ((640, 1024), BF16),
        ((640, 128), BF16),
        ((128, 128), BF16),
        ((128, 128), F32),
        ((128, 128), F32),
        ((128, 8, 128), BF16),
        ((32, 4, 8, 128), BF16),
        ((128, 8, 128), F32),
        ((4, 8, 128), BF16),
        ((8, 4, 8, 128), BF16),
        ((4, 8, 128), BF16),
        ((128, 8, 128), BF16),
    ]
    shapes = (
        jax.ShapeDtypeStruct((4, 8, 32, 128), BF16),
        jax.ShapeDtypeStruct((4, 8, 32, 128), F32),
        jax.ShapeDtypeStruct((128, 640), F32),
        jax.ShapeDtypeStruct((128, 128), F32),
        jax.ShapeDtypeStruct((2, 128), F32),
    )
    operands = [
        pltpu.with_memory_space_constraint(value, pltpu.HBM)
        for value in (
            pair.reshape(4, 8, 32, 128), gain_in.reshape(1, 128), in_weight,
            gain_out.reshape(1, 128), out_weight, out_grad.reshape(4, 8, 32, 128),
        )
    ]
    results = pl.pallas_call(
        kernel,
        out_shape=shapes,
        in_specs=[hbm] * 6,
        out_specs=[vmem] * 5,
        scratch_shapes=[pltpu.VMEM(shape, kind) for shape, kind in scratch]
        + [
            pltpu.SemaphoreType.DMA((6,)),
            pltpu.SemaphoreType.DMA((7,)),
            pltpu.SemaphoreType.DMA((7, 8)),
            pltpu.SemaphoreType.DMA((3,)),
            pltpu.SemaphoreType.DMA((3,)),
        ],
        compiler_params=pltpu.CompilerParams(
            collective_id=0, has_side_effects=True, vmem_limit_bytes=48 * 2**20
        ),
    )(*operands)
    update, pair_grad, in_weight_grad, out_weight_grad, gain_grad = pl.pallas_call(
        write_out,
        out_shape=shapes,
        in_specs=[vmem] * 5,
        out_specs=[hbm] * 5,
        scratch_shapes=[pltpu.SemaphoreType.DMA((5,))],
        compiler_params=pltpu.CompilerParams(vmem_limit_bytes=16 * 2**20),
    )(*results)
    return (
        update.reshape(32, 32, 128), pair_grad.reshape(32, 32, 128),
        in_weight_grad, out_weight_grad, gain_grad,
    )


def solution(mesh):
    return jax.shard_map(
        on_device,
        mesh=mesh,
        in_specs=(P("row", "col", None), P(), P(), P(), P(), P("row", "col", None)),
        out_specs=(P("row", "col", None), P("row", "col", None), P(), P(), P()),
        check_vma=False,
    )
```

```python
import jax
import jax.numpy as jnp
from jax import lax
from jax.experimental import pallas as pl
from jax.experimental.pallas import tpu as pltpu
from jax.sharding import PartitionSpec as P

EPS = 1e-05
MESH = pl.DeviceIdType.MESH
F32 = jnp.float32
BF16 = jnp.bfloat16
NT = (((1,), (1,)), ((), ()))
TN = (((0,), (0,)), ((), ()))


def dot(a, b, dims=(((1,), (0,)), ((), ()))):
    return lax.dot_general(a, b, dims, preferred_element_type=F32)


def swap_blocks(tiles):
    shape = tiles[0].shape
    flat = [t.reshape(-1, 128) for t in tiles]
    lane = lax.broadcasted_iota(jnp.int32, flat[0].shape, 1)
    low = lane < 64
    even = (lane // 32) % 2 == 0
    half = [None] * 4
    for q in range(2):
        a, b = flat[q], flat[q + 2]
        half[q] = jnp.where(low, a, pltpu.roll(b, 64, 1))
        half[q + 2] = jnp.where(low, pltpu.roll(a, 64, 1), b)
    out = [None] * 4
    for q in (0, 2):
        a, b = half[q], half[q + 1]
        out[q] = jnp.where(even, a, pltpu.roll(b, 32, 1))
        out[q + 1] = jnp.where(even, pltpu.roll(a, 96, 1), b)
    return [t.reshape(shape) for t in out]


def kernel(
    pair_h, gain_in_h, weight_h, gain_out_h, out_weight_h, out_grad_h,
    update_o, pair_grad_o, weight_grad_o, out_weight_grad_o, gain_grad_o,
    pair, weight, out_weight, out_grad, gain_in, gain_out,
    wide, sb0, rb0, sb1, rb1, edges, sb2, rb2, sb3, rb3, grad_mat, grad_far, sb4, rb4, sb6, rb6,
    normed, hat_in, rstd_in, gates, grad_po, grad_no, og_t, grad_p, w_t, ow_t, g_in, g_out,
    sb5, rb5, sums, plane_sum, planes, total_bf, final,
    load, send, recv, sib_send, sib_recv,
):
    row, col = lax.axis_index("row"), lax.axis_index("col")
    core, rx = lax.rem(row, 2), lax.div(row, 2)
    me = rx * 16 + col
    z = lax.rem(col, 8)
    spot = lax.div(col, 8) * 16 + row
    sibling = (rx * 2 + 1 - core, col)
    barrier = pltpu.get_barrier_semaphore()

    def partners(act):
        def line(dr, first):
            r = lax.rem(rx + dr, 8)

            def one(dc, carry):
                act(dr, r, lax.rem(col + dc, 16))
                return carry

            lax.fori_loop(first, 16, one, 0, unroll=True)

        def rest(dr, carry):
            line(dr, 0)
            return carry

        line(0, 1)
        lax.fori_loop(1, 8, rest, 0)

    def greet(dr, r, c):
        pl.semaphore_signal(barrier, inc=1, device_id=(r * 2 + core, c), device_id_type=MESH)

    loads = [
        pltpu.make_async_copy(source, target, load.at[i])
        for i, (source, target) in enumerate(
            [
                (pair_h, pair), (weight_h, weight), (out_weight_h, out_weight), (out_grad_h, out_grad),
                (gain_in_h, gain_in), (gain_out_h, gain_out),
            ]
        )
    ]
    for copy in loads:
        copy.start()
    partners(greet)

    def in_plane(d):
        p = lax.rem(spot + d, 32)
        return p, (lax.rem(p, 16), lax.div(p, 16) * 8 + z)

    def greet_plane(d, carry):
        pl.semaphore_signal(barrier, inc=1, device_id=in_plane(2 * d + 1)[1], device_id_type=MESH)
        return carry

    lax.fori_loop(0, 16, greet_plane, 0, unroll=True)

    def exchange(source, target, slot):
        def one(dr, r, c):
            pltpu.make_async_remote_copy(
                src_ref=source.at[r * 16 + c], dst_ref=target.at[me], send_sem=send.at[slot],
                recv_sem=recv.at[slot, dr], device_id=(r * 2 + core, c), device_id_type=MESH,
            ).start()

        partners(one)
        target[me] = source[me]

    def drain(buffer, count, semaphore):
        view = buffer.at[pl.ds(0, count)]
        pltpu.make_async_copy(view, view, semaphore).wait()

    def send_row(source, target, slot, dr, r, first):
        def one(dc, carry):
            c = lax.rem(col + dc, 16)
            pltpu.make_async_remote_copy(
                src_ref=source.at[r * 16 + c], dst_ref=target.at[me], send_sem=send.at[slot],
                recv_sem=recv.at[slot, dr], device_id=(r * 2 + core, c), device_id_type=MESH,
            ).start()
            return carry

        lax.fori_loop(first, 16, one, 0, unroll=True)

    def arrive(buffer, slot):
        drain(buffer, 15, recv.at[slot, 0])

        def one(dr, carry):
            drain(buffer, 16, recv.at[slot, dr])
            return carry

        lax.fori_loop(1, 8, one, 0)

    def to_sibling(source, target, slot):
        return pltpu.make_async_remote_copy(
            src_ref=source, dst_ref=target, send_sem=sib_send.at[slot], recv_sem=sib_recv.at[slot],
            device_id=sibling, device_id_type=MESH,
        )

    loads[4].wait()
    loads[5].wait()
    g_in[...] = jnp.broadcast_to(gain_in[...], (128, 128)).T
    g_out[...] = jnp.broadcast_to(gain_out[...], (128, 128)).T
    loads[0].wait()
    loads[1].wait()
    w_t[...] = weight[...].astype(F32).T.astype(BF16)
    for s in range(8):
        lanes = pl.ds(s * 128, 128)
        x = pair[:, s].reshape(128, 128).astype(F32).T
        centred = x - jnp.mean(x, axis=0, keepdims=True)
        rstd = lax.rsqrt(jnp.mean(centred * centred, axis=0, keepdims=True) + EPS)
        hat = centred * rstd
        hat_in[:, lanes] = hat
        rstd_in[:, lanes] = rstd
        n = (hat * g_in[...]).astype(BF16)
        normed[:, lanes] = n
        p = dot(w_t[pl.ds(0, 512)], n)
        s0, p1 = jax.nn.sigmoid(p[0:128]), p[128:256]
        s2, p3 = jax.nn.sigmoid(p[256:384]), p[384:512]
        gates[0, :, lanes] = s0
        gates[1, :, lanes] = p1
        gates[2, :, lanes] = s2
        gates[3, :, lanes] = p3
        wide[:, s, :] = s0 * p1
        wide[:, 8 + s, :] = s2 * p3
    sb1[...] = wide[:, 8:16, :].astype(BF16)
    sb0[...] = wide[:, 0:8, :].astype(BF16)

    pl.semaphore_wait(barrier, 143)
    exchange(sb1, rb1, 0)
    exchange(sb0, rb0, 8)

    loads[2].wait()
    loads[3].wait()
    ow_t[...] = out_weight[...].astype(F32).T.astype(BF16)
    for s in range(8):
        lanes = pl.ds(s * 128, 128)
        gate = jax.nn.sigmoid(dot(w_t[pl.ds(512, 128)], normed[:, lanes]))
        gates[4, :, lanes] = gate
        cotangent = out_grad[:, s].reshape(128, 128).astype(F32).T
        og_t[:, lanes] = cotangent
        gpo = (cotangent * gate).astype(BF16)
        grad_po[:, lanes] = gpo
        grad_no[:, lanes] = dot(out_weight[...], gpo)

    def side_of(slot, side):
        return edges[slot, side].reshape(256, 512)

    def place(slot):
        return core if slot == 0 else 1 - core

    def edge_rows(buffer, side, r):
        parts = []
        for g in range(4):
            parts.append(swap_blocks([buffer[r * 16 + 4 * g + q].astype(F32) for q in range(4)]))
        rows = [jnp.concatenate([parts[g][a] for g in range(4)], axis=1) for a in range(4)]
        edges[0, side, r] = jnp.concatenate(rows, axis=0).astype(BF16)
        to_sibling(edges.at[0, side, r], edges.at[1, side, r], side).start()

    def right_group(dr, carry):
        drain(rb1, 16, recv.at[0, dr])
        edge_rows(rb1, 1, lax.rem(rx + 8 - dr, 8))
        return carry

    drain(rb1, 15, recv.at[0, 0])
    edge_rows(rb1, 1, rx)
    lax.fori_loop(1, 8, right_group, 0)
    to_sibling(edges.at[0, 1], edges.at[1, 1], 1).wait_recv()

    def send_mixed(dr, r, first):
        edge_rows(rb0, 0, r)
        for slot in range(2):
            rows = dot(edges[0, 0, r], side_of(slot, 1), NT)
            for g in range(2):
                tiles = swap_blocks([rows[8 * a : 8 * a + 8, g * 128 : g * 128 + 128] for a in range(4)])
                for q in range(4):
                    sb2[r * 16 + 2 * (4 * g + q) + place(slot)] = tiles[q].astype(BF16)
        send_row(sb2, rb2, 1, dr, r, first)

    def mixed_group(dr, carry):
        drain(rb0, 16, recv.at[8, dr])
        send_mixed(dr, lax.rem(rx + 8 - dr, 8), 0)
        return carry

    drain(rb0, 15, recv.at[8, 0])
    send_mixed(0, rx, 1)
    rb2[me] = sb2[me]
    lax.fori_loop(1, 8, mixed_group, 0)
    arrive(rb2, 1)

    wide[:, 0:8, :] = rb2[...].astype(F32)
    gain_sum = jnp.zeros((128, 128), F32)
    for s in range(8):
        lanes = pl.ds(s * 128, 128)
        x = wide[:, s, :]
        centred = x - jnp.mean(x, axis=0, keepdims=True)
        rstd = lax.rsqrt(jnp.mean(centred * centred, axis=0, keepdims=True) + EPS)
        hat = centred * rstd
        gno = grad_no[:, lanes]
        gain_sum = gain_sum + gno * hat
        cot = gno * g_out[...]
        inner = jnp.mean(cot * hat, axis=0, keepdims=True)
        grad = rstd * (cot - jnp.mean(cot, axis=0, keepdims=True) - hat * inner)
        grad_no[:, lanes] = hat
        wide[:, 8 + s, :] = grad
    sb3[...] = wide[:, 8:16, :].astype(BF16)
    exchange(sb3, rb3, 2)

    gain_out_part = jnp.sum(gain_sum.T, axis=0, keepdims=True)
    for s in range(8):
        lanes = pl.ds(s * 128, 128)
        no = (grad_no[:, lanes] * g_out[...]).astype(BF16)
        grad_p[pl.ds(0, 128), lanes] = no
        po = dot(ow_t[...], no)
        gate = gates[4, :, lanes]
        update_o[:, s] = (gate * po).T.reshape(4, 32, 128).astype(BF16)
        grad_p[pl.ds(512, 128), lanes] = (og_t[:, lanes] * po * (gate * (1.0 - gate))).astype(BF16)

    def grad_rows(dr):
        r = lax.rem(rx + 8 - dr, 8)
        for slot in range(2):
            parts = []
            for g in range(2):
                parts.append(
                    swap_blocks([rb3[r * 16 + 2 * (4 * g + q) + place(slot)].astype(F32) for q in range(4)])
                )
            rows = [jnp.concatenate([parts[0][a], parts[1][a]], axis=1) for a in range(4)]
            grad_mat[slot, r] = jnp.concatenate(rows, axis=0).astype(BF16)
        to_sibling(grad_mat.at[1, r], grad_far.at[r], 2).start()

    def send_left(dr, first):
        r = lax.rem(rx + 8 - dr, 8)
        rows = dot(grad_mat[0, r], side_of(0, 1)) + dot(grad_mat[1, r], side_of(1, 1))
        for g in range(4):
            tiles = swap_blocks([rows[8 * a : 8 * a + 8, g * 128 : g * 128 + 128] for a in range(4)])
            for q in range(4):
                sb4[r * 16 + 4 * g + q] = tiles[q].astype(BF16)

        send_row(sb4, rb4, 3, dr, r, first)

    drain(sb3, 15, recv.at[2, 0])
    grad_rows(0)
    send_left(0, 1)
    rb4[me] = sb4[me]

    def grad_group(dr, carry):
        drain(sb3, 16, recv.at[2, dr])
        grad_rows(dr)
        send_left(dr, 0)
        return carry

    lax.fori_loop(1, 8, grad_group, 0)
    to_sibling(edges.at[0, 0], edges.at[1, 0], 0).wait_recv()
    near = grad_mat[0].reshape(256, 256)
    grad_right = dot(near, side_of(0, 0), TN)
    to_sibling(grad_mat.at[1], grad_far, 2).wait_recv()
    grad_right = (grad_right + dot(grad_far[...].reshape(256, 256), side_of(1, 0), TN)).reshape(8, 4, 8, 512)
    for g in range(4):
        tiles = swap_blocks([grad_right[:, a, :, g * 128 : g * 128 + 128] for a in range(4)])
        for q in range(4):
            sb6.reshape(8, 16, 8, 128)[:, 4 * g + q] = tiles[q].astype(BF16)
    exchange(sb6, rb6, 7)

    out_part = dot(grad_p[pl.ds(0, 128)], grad_po[...], NT)
    gate_part = dot(normed[...], grad_p[pl.ds(512, 128)], NT)
    sums[:, 4, :] = gate_part
    sums[:, 5, :] = out_part
    sums[:, 7, :] = jnp.broadcast_to(gain_out_part, (128, 128))

    def edge_grads(buffer, gate, r):
        first = pl.multiple_of(r * 16, 16)
        here = pl.ds(first, 16)
        wide[here, 0:8, :] = buffer[here].astype(F32)
        for s in range(8):
            lanes = pl.ds(s * 128, 128)
            sig, value = gates[gate, here, lanes], gates[gate + 1, here, lanes]
            grad = wide[here, s, :] * sig
            grad_p[pl.ds(128 * gate + first, 16), lanes] = (grad * value * (1.0 - sig)).astype(BF16)
            grad_p[pl.ds(128 * gate + 128 + first, 16), lanes] = grad.astype(BF16)

    def left_group(dr, carry):
        drain(rb4, 16, recv.at[3, dr])
        edge_grads(rb4, 0, lax.rem(rx + dr, 8))
        return carry

    def right_group(dr, carry):
        drain(rb6, 16, recv.at[7, dr])
        edge_grads(rb6, 2, lax.rem(rx + 8 - dr, 8))
        return carry

    drain(rb4, 15, recv.at[3, 0])
    edge_grads(rb4, 0, rx)
    lax.fori_loop(1, 8, left_group, 0)
    drain(rb6, 15, recv.at[7, 0])
    edge_grads(rb6, 2, rx)
    lax.fori_loop(1, 8, right_group, 0)
    gain_sum = jnp.zeros((128, 128), F32)
    for s in range(8):
        lanes = pl.ds(s * 128, 128)
        gni = dot(weight[...], grad_p[:, lanes])
        gain_sum = gain_sum + gni * hat_in[:, lanes]
        og_t[:, lanes] = gni
    gain_in_part = jnp.sum(gain_sum.T, axis=0, keepdims=True)
    in_part = dot(normed[...], grad_p[pl.ds(0, 512)], NT)
    for b in range(4):
        sums[:, b, :] = in_part[:, b * 128 : b * 128 + 128]
    sums[:, 6, :] = jnp.broadcast_to(gain_in_part, (128, 128))

    def along_plane(source, target, slot):
        def one(d, carry):
            p, device = in_plane(d)
            pltpu.make_async_remote_copy(
                src_ref=source(p), dst_ref=target, send_sem=send.at[slot], recv_sem=recv.at[slot, 0],
                device_id=device, device_id_type=MESH,
            ).start()
            return carry

        lax.fori_loop(1, 32, one, 0, unroll=True)

    def rows_of(p):
        return pl.ds(pl.multiple_of(p * 4, 4), 4)

    sb5[...] = sums[...].astype(BF16)
    along_plane(lambda p: sb5.at[rows_of(p)], rb5.at[spot], 4)
    rb5[spot] = sb5[rows_of(spot)]
    for s in range(8):
        lanes = pl.ds(s * 128, 128)
        hat = hat_in[:, lanes]
        cot = og_t[:, lanes] * g_in[...]
        inner = jnp.mean(cot * hat, axis=0, keepdims=True)
        grad = rstd_in[:, lanes] * (cot - jnp.mean(cot, axis=0, keepdims=True) - hat * inner)
        pair_grad_o[:, s] = grad.T.reshape(4, 32, 128)
    drain(rb5, 31, recv.at[4, 0])
    plane_sum[...] = jnp.sum(rb5[...].astype(F32), axis=0).astype(BF16)

    def along_z(d, carry):
        pltpu.make_async_remote_copy(
            src_ref=plane_sum, dst_ref=planes.at[z], send_sem=send.at[5], recv_sem=recv.at[5, 0],
            device_id=(row, lax.div(col, 8) * 8 + lax.rem(z + d, 8)), device_id_type=MESH,
        ).start()
        return carry

    lax.fori_loop(1, 8, along_z, 0, unroll=True)
    planes[z] = plane_sum[...]
    drain(planes, 7, recv.at[5, 0])
    total = jnp.sum(planes[...].astype(F32), axis=0)
    gain_grad_o[...] = total[0, 6:8]
    total_bf[...] = total.astype(BF16)
    along_plane(lambda p: total_bf, final.at[rows_of(spot)], 6)
    final[rows_of(spot)] = total_bf[...]
    drain(sb1, 127, send.at[0])
    drain(sb0, 127, send.at[8])
    drain(rb2, 127, send.at[1])
    drain(sb3, 127, send.at[2])
    drain(rb4, 127, send.at[3])
    drain(rb6, 127, send.at[7])
    drain(rb5, 31, send.at[4])
    drain(planes, 7, send.at[5])
    drain(rb5, 31, send.at[6])
    for side in range(2):
        to_sibling(edges.at[0, side], edges.at[1, side], side).wait_send()
    to_sibling(grad_mat.at[1], grad_far, 2).wait_send()
    drain(rb5, 31, recv.at[6, 0])
    sums[...] = final[...].astype(F32)
    for b in range(5):
        weight_grad_o[:, pl.ds(b * 128, 128)] = sums[:, b, :]
    out_weight_grad_o[...] = sums[:, 5, :]


def write_out(*refs):
    count = len(refs) // 2
    copies = [
        pltpu.make_async_copy(refs[i], refs[count + i], refs[-1].at[i]) for i in range(count)
    ]
    for copy in copies:
        copy.start()
    for copy in copies:
        copy.wait()


def on_device(pair, gain_in, in_weight, gain_out, out_weight, out_grad):
    vmem = pl.BlockSpec(memory_space=pltpu.VMEM)
    hbm = pl.BlockSpec(memory_space=pltpu.HBM)
    scratch = [
        ((4, 8, 32, 128), BF16),
        ((128, 640), BF16),
        ((128, 128), BF16),
        ((4, 8, 32, 128), BF16),
        ((1, 128), F32),
        ((1, 128), F32),
        ((128, 16, 128), F32),
        ((128, 8, 128), BF16),
        ((128, 8, 128), BF16),
        ((128, 8, 128), BF16),
        ((128, 8, 128), BF16),
        ((2, 2, 8, 32, 512), BF16),
        ((128, 8, 128), BF16),
        ((128, 8, 128), BF16),
        ((128, 8, 128), BF16),
        ((128, 8, 128), BF16),
        ((2, 8, 32, 256), BF16),
        ((8, 32, 256), BF16),
        ((128, 8, 128), BF16),
        ((128, 8, 128), BF16),
        ((128, 8, 128), BF16),
        ((128, 8, 128), BF16),
        ((128, 1024), BF16),
        ((128, 1024), F32),
        ((1, 1024), F32),
        ((5, 128, 1024), F32),
        ((128, 1024), BF16),
        ((128, 1024), F32),
        ((128, 1024), F32),
        ((640, 1024), BF16),
        ((640, 128), BF16),
        ((128, 128), BF16),
        ((128, 128), F32),
        ((128, 128), F32),
        ((128, 8, 128), BF16),
        ((32, 4, 8, 128), BF16),
        ((128, 8, 128), F32),
        ((4, 8, 128), BF16),
        ((8, 4, 8, 128), BF16),
        ((4, 8, 128), BF16),
        ((128, 8, 128), BF16),
    ]
    shapes = (
        jax.ShapeDtypeStruct((4, 8, 32, 128), BF16),
        jax.ShapeDtypeStruct((4, 8, 32, 128), F32),
        jax.ShapeDtypeStruct((128, 640), F32),
        jax.ShapeDtypeStruct((128, 128), F32),
        jax.ShapeDtypeStruct((2, 128), F32),
    )
    operands = [
        pltpu.with_memory_space_constraint(value, pltpu.HBM)
        for value in (
            pair.reshape(4, 8, 32, 128), gain_in.reshape(1, 128), in_weight,
            gain_out.reshape(1, 128), out_weight, out_grad.reshape(4, 8, 32, 128),
        )
    ]
    results = pl.pallas_call(
        kernel,
        out_shape=shapes,
        in_specs=[hbm] * 6,
        out_specs=[vmem] * 5,
        scratch_shapes=[pltpu.VMEM(shape, kind) for shape, kind in scratch]
        + [
            pltpu.SemaphoreType.DMA((6,)),
            pltpu.SemaphoreType.DMA((9,)),
            pltpu.SemaphoreType.DMA((9, 8)),
            pltpu.SemaphoreType.DMA((3,)),
            pltpu.SemaphoreType.DMA((3,)),
        ],
        compiler_params=pltpu.CompilerParams(
            collective_id=0, has_side_effects=True, vmem_limit_bytes=48 * 2**20
        ),
    )(*operands)
    update, pair_grad, in_weight_grad, out_weight_grad, gain_grad = pl.pallas_call(
        write_out,
        out_shape=shapes,
        in_specs=[vmem] * 5,
        out_specs=[hbm] * 5,
        scratch_shapes=[pltpu.SemaphoreType.DMA((5,))],
        compiler_params=pltpu.CompilerParams(vmem_limit_bytes=16 * 2**20),
    )(*results)
    return (
        update.reshape(32, 32, 128), pair_grad.reshape(32, 32, 128),
        in_weight_grad, out_weight_grad, gain_grad,
    )


def solution(mesh):
    return jax.shard_map(
        on_device,
        mesh=mesh,
        in_specs=(P("row", "col", None), P(), P(), P(), P(), P("row", "col", None)),
        out_specs=(P("row", "col", None), P("row", "col", None), P(), P(), P()),
        check_vma=False,
    )
```

```python
import jax
import jax.numpy as jnp
from jax import lax
from jax.experimental import pallas as pl
from jax.experimental.pallas import tpu as pltpu
from jax.sharding import PartitionSpec as P

EPS = 1e-05
SPAN = 2
MESH = pl.DeviceIdType.MESH
F32 = jnp.float32
BF16 = jnp.bfloat16
NT = (((1,), (1,)), ((), ()))
TN = (((0,), (0,)), ((), ()))


def dot(a, b, dims=(((1,), (0,)), ((), ()))):
    return lax.dot_general(a, b, dims, preferred_element_type=F32)


def swap_blocks(tiles):
    shape = tiles[0].shape
    flat = [t.reshape(-1, 128) for t in tiles]
    lane = lax.broadcasted_iota(jnp.int32, flat[0].shape, 1)
    low = lane < 64
    even = (lane // 32) % 2 == 0
    half = [None] * 4
    for q in range(2):
        a, b = flat[q], flat[q + 2]
        half[q] = jnp.where(low, a, pltpu.roll(b, 64, 1))
        half[q + 2] = jnp.where(low, pltpu.roll(a, 64, 1), b)
    out = [None] * 4
    for q in (0, 2):
        a, b = half[q], half[q + 1]
        out[q] = jnp.where(even, a, pltpu.roll(b, 32, 1))
        out[q + 1] = jnp.where(even, pltpu.roll(a, 96, 1), b)
    return [t.reshape(shape) for t in out]


def kernel(
    pair_h, gain_in_h, weight_h, gain_out_h, out_weight_h, out_grad_h,
    update_o, pair_grad_o, weight_grad_o, out_weight_grad_o, gain_grad_o,
    pair, weight, out_weight, out_grad, gain_in, gain_out,
    wide, sb0, rb0, sb1, rb1, edges, right_t, sb2, rb2, sb3, rb3, grad_mat, grad_far, sb4, rb4, sb6, rb6,
    normed, hat_in, rstd_in, gates, grad_po, grad_no, og_t, grad_p, w_t, ow_t, g_in, g_out,
    sb5, rb5, sums, plane_sum, planes, total_bf, final,
    load, send, recv, sib_send, sib_recv,
):
    row, col = lax.axis_index("row"), lax.axis_index("col")
    core, rx = lax.rem(row, 2), lax.div(row, 2)
    me = rx * 16 + col
    z = lax.rem(col, 8)
    spot = lax.div(col, 8) * 16 + row
    sibling = (rx * 2 + 1 - core, col)
    barrier = pltpu.get_barrier_semaphore()

    def partners(act):
        def line(dr, first):
            r = lax.rem(rx + dr, 8)

            def one(dc, carry):
                act(dr, r, lax.rem(col + dc, 16))
                return carry

            lax.fori_loop(first, 16, one, 0, unroll=True)

        def rest(dr, carry):
            line(dr, 0)
            return carry

        line(0, 1)
        lax.fori_loop(1, 8, rest, 0)

    def greet(dr, r, c):
        pl.semaphore_signal(barrier, inc=1, device_id=(r * 2 + core, c), device_id_type=MESH)

    loads = [
        pltpu.make_async_copy(source, target, load.at[i])
        for i, (source, target) in enumerate(
            [
                (pair_h, pair), (weight_h, weight), (out_weight_h, out_weight), (out_grad_h, out_grad),
                (gain_in_h, gain_in), (gain_out_h, gain_out),
            ]
        )
    ]
    for copy in loads:
        copy.start()
    partners(greet)

    def in_plane(d):
        p = lax.rem(spot + d, 32)
        return p, (lax.rem(p, 16), lax.div(p, 16) * 8 + z)

    def greet_plane(d, carry):
        pl.semaphore_signal(barrier, inc=1, device_id=in_plane(2 * d + 1)[1], device_id_type=MESH)
        return carry

    lax.fori_loop(0, 16, greet_plane, 0, unroll=True)

    def exchange(source, target, slot):
        def one(dr, r, c):
            pltpu.make_async_remote_copy(
                src_ref=source.at[r * 16 + c], dst_ref=target.at[me], send_sem=send.at[slot],
                recv_sem=recv.at[slot, dr], device_id=(r * 2 + core, c), device_id_type=MESH,
            ).start()

        partners(one)
        target[me] = source[me]

    def drain(buffer, count, semaphore):
        view = buffer.at[pl.ds(0, count)]
        pltpu.make_async_copy(view, view, semaphore).wait()

    def send_row(source, target, slot, dr, r, first):
        def one(dc, carry):
            c = lax.rem(col + dc, 16)
            pltpu.make_async_remote_copy(
                src_ref=source.at[r * 16 + c], dst_ref=target.at[me], send_sem=send.at[slot],
                recv_sem=recv.at[slot, dr], device_id=(r * 2 + core, c), device_id_type=MESH,
            ).start()
            return carry

        lax.fori_loop(first, 16, one, 0, unroll=True)

    def arrive(buffer, slot):
        drain(buffer, 15, recv.at[slot, 0])

        def one(dr, carry):
            drain(buffer, 16, recv.at[slot, dr])
            return carry

        lax.fori_loop(1, 8, one, 0)

    def to_sibling(source, target, slot):
        return pltpu.make_async_remote_copy(
            src_ref=source, dst_ref=target, send_sem=sib_send.at[slot], recv_sem=sib_recv.at[slot],
            device_id=sibling, device_id_type=MESH,
        )

    loads[4].wait()
    loads[5].wait()
    g_in[...] = jnp.broadcast_to(gain_in[...], (128, 128)).T
    g_out[...] = jnp.broadcast_to(gain_out[...], (128, 128)).T
    loads[0].wait()
    loads[1].wait()
    w_t[...] = weight[...].astype(F32).T.astype(BF16)
    for s in range(8):
        lanes = pl.ds(s * 128, 128)
        x = pair[:, s].reshape(128, 128).astype(F32).T
        centred = x - jnp.mean(x, axis=0, keepdims=True)
        rstd = lax.rsqrt(jnp.mean(centred * centred, axis=0, keepdims=True) + EPS)
        hat = centred * rstd
        hat_in[:, lanes] = hat
        rstd_in[:, lanes] = rstd
        n = (hat * g_in[...]).astype(BF16)
        normed[:, lanes] = n
        p = dot(w_t[pl.ds(0, 512)], n)
        s0, p1 = jax.nn.sigmoid(p[0:128]), p[128:256]
        s2, p3 = jax.nn.sigmoid(p[256:384]), p[384:512]
        gates[0, :, lanes] = s0
        gates[1, :, lanes] = p1
        gates[2, :, lanes] = s2
        gates[3, :, lanes] = p3
        wide[:, s, :] = s0 * p1
        wide[:, 8 + s, :] = s2 * p3
    sb1[...] = wide[:, 8:16, :].astype(BF16)
    sb0[...] = wide[:, 0:8, :].astype(BF16)

    pl.semaphore_wait(barrier, 143)
    exchange(sb1, rb1, 0)
    exchange(sb0, rb0, 8)

    def side_of(slot, side):
        return edges[slot, side].reshape(256, 512)

    def place(slot):
        return core if slot == 0 else 1 - core

    def edge_rows(buffer, side, r):
        parts = []
        for g in range(4):
            parts.append(swap_blocks([buffer[r * 16 + 4 * g + q].astype(F32) for q in range(4)]))
        rows = [jnp.concatenate([parts[g][a] for g in range(4)], axis=1) for a in range(4)]
        edges[0, side, r] = jnp.concatenate(rows, axis=0).astype(BF16)
        to_sibling(edges.at[0, side, r], edges.at[1, side, r], side).start()

    def right_group(dr, carry):
        drain(rb1, 16, recv.at[0, dr])
        edge_rows(rb1, 1, lax.rem(rx + 8 - dr, 8))
        return carry

    drain(rb1, 15, recv.at[0, 0])
    edge_rows(rb1, 1, rx)
    lax.fori_loop(1, 8, right_group, 0)
    to_sibling(edges.at[0, 1], edges.at[1, 1], 1).wait_recv()

    for slot in range(2):
        right_t[:, pl.ds(256 * slot, 256)] = side_of(slot, 1).astype(F32).T.astype(BF16)

    def behind(dr):
        return lax.rem(rx + 8 - dr, 8)

    def send_mixed(start, first):
        near = [(start + i, behind(start + i)) for i in range(SPAN)]
        for i, (dr, r) in enumerate(near):
            drain(rb0, 15 if first and i == 0 else 16, recv.at[8, dr])
            edge_rows(rb0, 0, r)
        every = dot(jnp.concatenate([edges[0, 0, r] for _, r in near], axis=0), right_t[...])
        for i, (dr, r) in enumerate(near):
            rows = every[32 * i : 32 * i + 32]
            for slot in range(2):
                for g in range(2):
                    lanes = slice(slot * 256 + g * 128, slot * 256 + g * 128 + 128)
                    tiles = swap_blocks([rows[8 * a : 8 * a + 8, lanes] for a in range(4)])
                    for q in range(4):
                        sb2[r * 16 + 2 * (4 * g + q) + place(slot)] = tiles[q].astype(BF16)
            send_row(sb2, rb2, 1, dr, r, 1 if first and i == 0 else 0)

    def mixed_group(step, carry):
        send_mixed(step * SPAN, False)
        return carry

    send_mixed(0, True)
    rb2[me] = sb2[me]
    lax.fori_loop(1, 8 // SPAN, mixed_group, 0)

    loads[2].wait()
    loads[3].wait()
    ow_t[...] = out_weight[...].astype(F32).T.astype(BF16)
    for s in range(8):
        lanes = pl.ds(s * 128, 128)
        gate = jax.nn.sigmoid(dot(w_t[pl.ds(512, 128)], normed[:, lanes]))
        gates[4, :, lanes] = gate
        cotangent = out_grad[:, s].reshape(128, 128).astype(F32).T
        og_t[:, lanes] = cotangent
        gpo = (cotangent * gate).astype(BF16)
        grad_po[:, lanes] = gpo
        grad_no[:, lanes] = dot(out_weight[...], gpo)

    arrive(rb2, 1)

    wide[:, 0:8, :] = rb2[...].astype(F32)
    gain_sum = jnp.zeros((128, 128), F32)
    for s in range(8):
        lanes = pl.ds(s * 128, 128)
        x = wide[:, s, :]
        centred = x - jnp.mean(x, axis=0, keepdims=True)
        rstd = lax.rsqrt(jnp.mean(centred * centred, axis=0, keepdims=True) + EPS)
        hat = centred * rstd
        gno = grad_no[:, lanes]
        gain_sum = gain_sum + gno * hat
        cot = gno * g_out[...]
        inner = jnp.mean(cot * hat, axis=0, keepdims=True)
        grad = rstd * (cot - jnp.mean(cot, axis=0, keepdims=True) - hat * inner)
        grad_no[:, lanes] = hat
        wide[:, 8 + s, :] = grad
    sb3[...] = wide[:, 8:16, :].astype(BF16)
    exchange(sb3, rb3, 2)

    def grad_rows(dr):
        r = lax.rem(rx + 8 - dr, 8)
        for slot in range(2):
            parts = []
            for g in range(2):
                parts.append(
                    swap_blocks([rb3[r * 16 + 2 * (4 * g + q) + place(slot)].astype(F32) for q in range(4)])
                )
            rows = [jnp.concatenate([parts[0][a], parts[1][a]], axis=1) for a in range(4)]
            grad_mat[slot, r] = jnp.concatenate(rows, axis=0).astype(BF16)
        to_sibling(grad_mat.at[1, r], grad_far.at[r], 2).start()

    def send_left(start, first):
        near = [(start + i, behind(start + i)) for i in range(SPAN)]
        for i, (dr, r) in enumerate(near):
            drain(sb3, 15 if first and i == 0 else 16, recv.at[2, dr])
            grad_rows(dr)
        every = sum(
            dot(jnp.concatenate([grad_mat[slot, r] for _, r in near], axis=0), side_of(slot, 1))
            for slot in range(2)
        )
        for i, (dr, r) in enumerate(near):
            rows = every[32 * i : 32 * i + 32]
            for g in range(4):
                tiles = swap_blocks([rows[8 * a : 8 * a + 8, g * 128 : g * 128 + 128] for a in range(4)])
                for q in range(4):
                    sb4[r * 16 + 4 * g + q] = tiles[q].astype(BF16)
            send_row(sb4, rb4, 3, dr, r, 1 if first and i == 0 else 0)

    def left_rows(step, carry):
        send_left(step * SPAN, False)
        return carry

    send_left(0, True)
    rb4[me] = sb4[me]
    lax.fori_loop(1, 8 // SPAN, left_rows, 0)
    to_sibling(edges.at[0, 0], edges.at[1, 0], 0).wait_recv()
    mine = grad_mat[0].reshape(256, 256)
    grad_right = dot(mine, side_of(0, 0), TN)
    to_sibling(grad_mat.at[1], grad_far, 2).wait_recv()
    grad_right = (grad_right + dot(grad_far[...].reshape(256, 256), side_of(1, 0), TN)).reshape(8, 4, 8, 512)
    for g in range(4):
        tiles = swap_blocks([grad_right[:, a, :, g * 128 : g * 128 + 128] for a in range(4)])
        for q in range(4):
            sb6.reshape(8, 16, 8, 128)[:, 4 * g + q] = tiles[q].astype(BF16)
    exchange(sb6, rb6, 7)

    gain_out_part = jnp.sum(gain_sum.T, axis=0, keepdims=True)
    for s in range(8):
        lanes = pl.ds(s * 128, 128)
        no = (grad_no[:, lanes] * g_out[...]).astype(BF16)
        grad_p[pl.ds(0, 128), lanes] = no
        po = dot(ow_t[...], no)
        gate = gates[4, :, lanes]
        update_o[:, s] = (gate * po).T.reshape(4, 32, 128).astype(BF16)
        grad_p[pl.ds(512, 128), lanes] = (og_t[:, lanes] * po * (gate * (1.0 - gate))).astype(BF16)
    out_part = dot(grad_p[pl.ds(0, 128)], grad_po[...], NT)
    gate_part = dot(normed[...], grad_p[pl.ds(512, 128)], NT)
    sums[:, 4, :] = gate_part
    sums[:, 5, :] = out_part
    sums[:, 7, :] = jnp.broadcast_to(gain_out_part, (128, 128))

    def edge_grads(buffer, gate, r):
        first = pl.multiple_of(r * 16, 16)
        here = pl.ds(first, 16)
        wide[here, 0:8, :] = buffer[here].astype(F32)
        for s in range(8):
            lanes = pl.ds(s * 128, 128)
            sig, value = gates[gate, here, lanes], gates[gate + 1, here, lanes]
            grad = wide[here, s, :] * sig
            grad_p[pl.ds(128 * gate + first, 16), lanes] = (grad * value * (1.0 - sig)).astype(BF16)
            grad_p[pl.ds(128 * gate + 128 + first, 16), lanes] = grad.astype(BF16)

    def left_group(dr, carry):
        drain(rb4, 16, recv.at[3, dr])
        edge_grads(rb4, 0, lax.rem(rx + dr, 8))
        return carry

    def right_group(dr, carry):
        drain(rb6, 16, recv.at[7, dr])
        edge_grads(rb6, 2, lax.rem(rx + 8 - dr, 8))
        return carry

    drain(rb4, 15, recv.at[3, 0])
    edge_grads(rb4, 0, rx)
    lax.fori_loop(1, 8, left_group, 0)
    drain(rb6, 15, recv.at[7, 0])
    edge_grads(rb6, 2, rx)
    lax.fori_loop(1, 8, right_group, 0)
    gain_sum = jnp.zeros((128, 128), F32)
    for s in range(8):
        lanes = pl.ds(s * 128, 128)
        gni = dot(weight[...], grad_p[:, lanes])
        gain_sum = gain_sum + gni * hat_in[:, lanes]
        og_t[:, lanes] = gni
    gain_in_part = jnp.sum(gain_sum.T, axis=0, keepdims=True)
    in_part = dot(normed[...], grad_p[pl.ds(0, 512)], NT)
    for b in range(4):
        sums[:, b, :] = in_part[:, b * 128 : b * 128 + 128]
    sums[:, 6, :] = jnp.broadcast_to(gain_in_part, (128, 128))

    def along_plane(source, target, slot):
        def one(d, carry):
            p, device = in_plane(d)
            pltpu.make_async_remote_copy(
                src_ref=source(p), dst_ref=target, send_sem=send.at[slot], recv_sem=recv.at[slot, 0],
                device_id=device, device_id_type=MESH,
            ).start()
            return carry

        lax.fori_loop(1, 32, one, 0, unroll=True)

    def rows_of(p):
        return pl.ds(pl.multiple_of(p * 4, 4), 4)

    sb5[...] = sums[...].astype(BF16)
    along_plane(lambda p: sb5.at[rows_of(p)], rb5.at[spot], 4)
    rb5[spot] = sb5[rows_of(spot)]
    for s in range(8):
        lanes = pl.ds(s * 128, 128)
        hat = hat_in[:, lanes]
        cot = og_t[:, lanes] * g_in[...]
        inner = jnp.mean(cot * hat, axis=0, keepdims=True)
        grad = rstd_in[:, lanes] * (cot - jnp.mean(cot, axis=0, keepdims=True) - hat * inner)
        pair_grad_o[:, s] = grad.T.reshape(4, 32, 128)
    drain(rb5, 31, recv.at[4, 0])
    plane_sum[...] = jnp.sum(rb5[...].astype(F32), axis=0).astype(BF16)

    def along_z(d, carry):
        pltpu.make_async_remote_copy(
            src_ref=plane_sum, dst_ref=planes.at[z], send_sem=send.at[5], recv_sem=recv.at[5, 0],
            device_id=(row, lax.div(col, 8) * 8 + lax.rem(z + d, 8)), device_id_type=MESH,
        ).start()
        return carry

    lax.fori_loop(1, 8, along_z, 0, unroll=True)
    planes[z] = plane_sum[...]
    drain(planes, 7, recv.at[5, 0])
    total = jnp.sum(planes[...].astype(F32), axis=0)
    gain_grad_o[...] = total[0, 6:8]
    total_bf[...] = total.astype(BF16)
    along_plane(lambda p: total_bf, final.at[rows_of(spot)], 6)
    final[rows_of(spot)] = total_bf[...]
    drain(sb1, 127, send.at[0])
    drain(sb0, 127, send.at[8])
    drain(rb2, 127, send.at[1])
    drain(sb3, 127, send.at[2])
    drain(rb4, 127, send.at[3])
    drain(rb6, 127, send.at[7])
    drain(rb5, 31, send.at[4])
    drain(planes, 7, send.at[5])
    drain(rb5, 31, send.at[6])
    for side in range(2):
        to_sibling(edges.at[0, side], edges.at[1, side], side).wait_send()
    to_sibling(grad_mat.at[1], grad_far, 2).wait_send()
    drain(rb5, 31, recv.at[6, 0])
    sums[...] = final[...].astype(F32)
    for b in range(5):
        weight_grad_o[:, pl.ds(b * 128, 128)] = sums[:, b, :]
    out_weight_grad_o[...] = sums[:, 5, :]


def write_out(*refs):
    count = len(refs) // 2
    copies = [
        pltpu.make_async_copy(refs[i], refs[count + i], refs[-1].at[i]) for i in range(count)
    ]
    for copy in copies:
        copy.start()
    for copy in copies:
        copy.wait()


def on_device(pair, gain_in, in_weight, gain_out, out_weight, out_grad):
    vmem = pl.BlockSpec(memory_space=pltpu.VMEM)
    hbm = pl.BlockSpec(memory_space=pltpu.HBM)
    scratch = [
        ((4, 8, 32, 128), BF16),
        ((128, 640), BF16),
        ((128, 128), BF16),
        ((4, 8, 32, 128), BF16),
        ((1, 128), F32),
        ((1, 128), F32),
        ((128, 16, 128), F32),
        ((128, 8, 128), BF16),
        ((128, 8, 128), BF16),
        ((128, 8, 128), BF16),
        ((128, 8, 128), BF16),
        ((2, 2, 8, 32, 512), BF16),
        ((512, 512), BF16),
        ((128, 8, 128), BF16),
        ((128, 8, 128), BF16),
        ((128, 8, 128), BF16),
        ((128, 8, 128), BF16),
        ((2, 8, 32, 256), BF16),
        ((8, 32, 256), BF16),
        ((128, 8, 128), BF16),
        ((128, 8, 128), BF16),
        ((128, 8, 128), BF16),
        ((128, 8, 128), BF16),
        ((128, 1024), BF16),
        ((128, 1024), F32),
        ((1, 1024), F32),
        ((5, 128, 1024), F32),
        ((128, 1024), BF16),
        ((128, 1024), F32),
        ((128, 1024), F32),
        ((640, 1024), BF16),
        ((640, 128), BF16),
        ((128, 128), BF16),
        ((128, 128), F32),
        ((128, 128), F32),
        ((128, 8, 128), BF16),
        ((32, 4, 8, 128), BF16),
        ((128, 8, 128), F32),
        ((4, 8, 128), BF16),
        ((8, 4, 8, 128), BF16),
        ((4, 8, 128), BF16),
        ((128, 8, 128), BF16),
    ]
    shapes = (
        jax.ShapeDtypeStruct((4, 8, 32, 128), BF16),
        jax.ShapeDtypeStruct((4, 8, 32, 128), F32),
        jax.ShapeDtypeStruct((128, 640), F32),
        jax.ShapeDtypeStruct((128, 128), F32),
        jax.ShapeDtypeStruct((2, 128), F32),
    )
    operands = [
        pltpu.with_memory_space_constraint(value, pltpu.HBM)
        for value in (
            pair.reshape(4, 8, 32, 128), gain_in.reshape(1, 128), in_weight,
            gain_out.reshape(1, 128), out_weight, out_grad.reshape(4, 8, 32, 128),
        )
    ]
    results = pl.pallas_call(
        kernel,
        out_shape=shapes,
        in_specs=[hbm] * 6,
        out_specs=[vmem] * 5,
        scratch_shapes=[pltpu.VMEM(shape, kind) for shape, kind in scratch]
        + [
            pltpu.SemaphoreType.DMA((6,)),
            pltpu.SemaphoreType.DMA((9,)),
            pltpu.SemaphoreType.DMA((9, 8)),
            pltpu.SemaphoreType.DMA((3,)),
            pltpu.SemaphoreType.DMA((3,)),
        ],
        compiler_params=pltpu.CompilerParams(
            collective_id=0, has_side_effects=True, vmem_limit_bytes=48 * 2**20
        ),
    )(*operands)
    update, pair_grad, in_weight_grad, out_weight_grad, gain_grad = pl.pallas_call(
        write_out,
        out_shape=shapes,
        in_specs=[vmem] * 5,
        out_specs=[hbm] * 5,
        scratch_shapes=[pltpu.SemaphoreType.DMA((5,))],
        compiler_params=pltpu.CompilerParams(vmem_limit_bytes=16 * 2**20),
    )(*results)
    return (
        update.reshape(32, 32, 128), pair_grad.reshape(32, 32, 128),
        in_weight_grad, out_weight_grad, gain_grad,
    )


def solution(mesh):
    return jax.shard_map(
        on_device,
        mesh=mesh,
        in_specs=(P("row", "col", None), P(), P(), P(), P(), P("row", "col", None)),
        out_specs=(P("row", "col", None), P("row", "col", None), P(), P(), P()),
        check_vma=False,
    )
```

```python
import jax
import jax.numpy as jnp
from jax import lax
from jax.experimental import pallas as pl
from jax.experimental.pallas import tpu as pltpu
from jax.sharding import PartitionSpec as P

EPS = 1e-05
SPAN = 2
MESH = pl.DeviceIdType.MESH
F32 = jnp.float32
BF16 = jnp.bfloat16
NT = (((1,), (1,)), ((), ()))
TN = (((0,), (0,)), ((), ()))


def dot(a, b, dims=(((1,), (0,)), ((), ()))):
    return lax.dot_general(a, b, dims, preferred_element_type=F32)


def swap_blocks(tiles):
    shape = tiles[0].shape
    flat = [t.reshape(-1, 128) for t in tiles]
    lane = lax.broadcasted_iota(jnp.int32, flat[0].shape, 1)
    low = lane < 64
    even = (lane // 32) % 2 == 0
    half = [None] * 4
    for q in range(2):
        a, b = flat[q], flat[q + 2]
        half[q] = jnp.where(low, a, pltpu.roll(b, 64, 1))
        half[q + 2] = jnp.where(low, pltpu.roll(a, 64, 1), b)
    out = [None] * 4
    for q in (0, 2):
        a, b = half[q], half[q + 1]
        out[q] = jnp.where(even, a, pltpu.roll(b, 32, 1))
        out[q + 1] = jnp.where(even, pltpu.roll(a, 96, 1), b)
    return [t.reshape(shape) for t in out]


def kernel(
    pair_h, gain_in_h, weight_h, gain_out_h, out_weight_h, out_grad_h,
    update_o, pair_grad_o, weight_grad_o, out_weight_grad_o, gain_grad_o,
    pair, weight, out_weight, out_grad, gain_in, gain_out,
    wide, sb0, rb0, sb1, rb1, edges, right_t, sb2, rb2, sb3, rb3, grad_mat, grad_far, sb4, rb4, sb6, rb6,
    normed, hat_in, rstd_in, gates, grad_po, grad_no, og_t, grad_p, w_t, ow_t, g_in, g_out,
    sb5, rb5, sums, plane_sum, planes, total_bf, final,
    load, send, recv, sib_send, sib_recv,
):
    row, col = lax.axis_index("row"), lax.axis_index("col")
    core, rx = lax.rem(row, 2), lax.div(row, 2)
    me = rx * 16 + col
    z = lax.rem(col, 8)
    spot = lax.div(col, 8) * 16 + row
    sibling = (rx * 2 + 1 - core, col)
    barrier = pltpu.get_barrier_semaphore()

    def partners(act):
        def line(dr, first):
            r = lax.rem(rx + dr, 8)

            def one(dc, carry):
                act(dr, r, lax.rem(col + dc, 16))
                return carry

            lax.fori_loop(first, 16, one, 0, unroll=True)

        def rest(dr, carry):
            line(dr, 0)
            return carry

        line(0, 1)
        lax.fori_loop(1, 8, rest, 0)

    def greet_far_first():
        x, y = lax.div(rx, 2), lax.div(col, 8) * 2 + lax.rem(rx, 2)
        xs = [lax.rem(x + 2 + i, 4) * 4 + core for i in range(4)]
        ys = [lax.rem(y + 2 + i, 4) for i in range(4)]
        lines = [(lax.rem(v, 2) * 2, lax.div(v, 2) * 8) for v in ys]
        for pair_z in ((4,), (3, 5), (2, 6), (1, 7), (0,)):
            for k in range(16):
                if pair_z == (0,) and k == 10:
                    continue
                r, c = xs[k // 4] + lines[k % 4][0], lines[k % 4][1]
                for dz in pair_z:
                    device = (r, c + lax.rem(z + dz, 8))
                    pl.semaphore_signal(barrier, inc=1, device_id=device, device_id_type=MESH)

    loads = [
        pltpu.make_async_copy(source, target, load.at[i])
        for i, (source, target) in enumerate(
            [
                (pair_h, pair), (weight_h, weight), (out_weight_h, out_weight), (out_grad_h, out_grad),
                (gain_in_h, gain_in), (gain_out_h, gain_out),
            ]
        )
    ]
    for copy in loads:
        copy.start()
    greet_far_first()

    def in_plane(d):
        p = lax.rem(spot + d, 32)
        return p, (lax.rem(p, 16), lax.div(p, 16) * 8 + z)

    def greet_plane(d, carry):
        pl.semaphore_signal(barrier, inc=1, device_id=in_plane(2 * d + 1)[1], device_id_type=MESH)
        return carry

    lax.fori_loop(0, 16, greet_plane, 0, unroll=True)

    def exchange(source, target, slot):
        def one(dr, r, c):
            pltpu.make_async_remote_copy(
                src_ref=source.at[r * 16 + c], dst_ref=target.at[me], send_sem=send.at[slot],
                recv_sem=recv.at[slot, dr], device_id=(r * 2 + core, c), device_id_type=MESH,
            ).start()

        partners(one)
        target[me] = source[me]

    def drain(buffer, count, semaphore):
        view = buffer.at[pl.ds(0, count)]
        pltpu.make_async_copy(view, view, semaphore).wait()

    def send_row(source, target, slot, dr, r, first):
        def one(dc, carry):
            c = lax.rem(col + dc, 16)
            pltpu.make_async_remote_copy(
                src_ref=source.at[r * 16 + c], dst_ref=target.at[me], send_sem=send.at[slot],
                recv_sem=recv.at[slot, dr], device_id=(r * 2 + core, c), device_id_type=MESH,
            ).start()
            return carry

        lax.fori_loop(first, 16, one, 0, unroll=True)

    def arrive(buffer, slot):
        drain(buffer, 15, recv.at[slot, 0])

        def one(dr, carry):
            drain(buffer, 16, recv.at[slot, dr])
            return carry

        lax.fori_loop(1, 8, one, 0)

    def to_sibling(source, target, slot):
        return pltpu.make_async_remote_copy(
            src_ref=source, dst_ref=target, send_sem=sib_send.at[slot], recv_sem=sib_recv.at[slot],
            device_id=sibling, device_id_type=MESH,
        )

    loads[4].wait()
    loads[5].wait()
    g_in[...] = jnp.broadcast_to(gain_in[...], (128, 128)).T
    g_out[...] = jnp.broadcast_to(gain_out[...], (128, 128)).T
    loads[0].wait()
    loads[1].wait()
    w_t[...] = weight[...].astype(F32).T.astype(BF16)
    for s in range(8):
        lanes = pl.ds(s * 128, 128)
        x = pair[:, s].reshape(128, 128).astype(F32).T
        centred = x - jnp.mean(x, axis=0, keepdims=True)
        rstd = lax.rsqrt(jnp.mean(centred * centred, axis=0, keepdims=True) + EPS)
        hat = centred * rstd
        hat_in[:, lanes] = hat
        rstd_in[:, lanes] = rstd
        n = (hat * g_in[...]).astype(BF16)
        normed[:, lanes] = n
        p = dot(w_t[pl.ds(0, 512)], n)
        s0, p1 = jax.nn.sigmoid(p[0:128]), p[128:256]
        s2, p3 = jax.nn.sigmoid(p[256:384]), p[384:512]
        gates[0, :, lanes] = s0
        gates[1, :, lanes] = p1
        gates[2, :, lanes] = s2
        gates[3, :, lanes] = p3
        wide[:, s, :] = s0 * p1
        wide[:, 8 + s, :] = s2 * p3
    sb1[...] = wide[:, 8:16, :].astype(BF16)
    sb0[...] = wide[:, 0:8, :].astype(BF16)

    pl.semaphore_wait(barrier, 143)
    exchange(sb1, rb1, 0)
    exchange(sb0, rb0, 8)

    def side_of(slot, side):
        return edges[slot, side].reshape(256, 512)

    def place(slot):
        return core if slot == 0 else 1 - core

    def edge_rows(buffer, side, r):
        parts = []
        for g in range(4):
            parts.append(swap_blocks([buffer[r * 16 + 4 * g + q].astype(F32) for q in range(4)]))
        rows = [jnp.concatenate([parts[g][a] for g in range(4)], axis=1) for a in range(4)]
        edges[0, side, r] = jnp.concatenate(rows, axis=0).astype(BF16)
        to_sibling(edges.at[0, side, r], edges.at[1, side, r], side).start()

    def right_group(dr, carry):
        drain(rb1, 16, recv.at[0, dr])
        edge_rows(rb1, 1, lax.rem(rx + 8 - dr, 8))
        return carry

    drain(rb1, 15, recv.at[0, 0])
    edge_rows(rb1, 1, rx)
    lax.fori_loop(1, 8, right_group, 0)
    to_sibling(edges.at[0, 1], edges.at[1, 1], 1).wait_recv()

    for slot in range(2):
        right_t[:, pl.ds(256 * slot, 256)] = side_of(slot, 1).astype(F32).T.astype(BF16)

    def behind(dr):
        return lax.rem(rx + 8 - dr, 8)

    def send_mixed(start, first):
        near = [(start + i, behind(start + i)) for i in range(SPAN)]
        for i, (dr, r) in enumerate(near):
            drain(rb0, 15 if first and i == 0 else 16, recv.at[8, dr])
            edge_rows(rb0, 0, r)
        every = dot(jnp.concatenate([edges[0, 0, r] for _, r in near], axis=0), right_t[...])
        for i, (dr, r) in enumerate(near):
            rows = every[32 * i : 32 * i + 32]
            for slot in range(2):
                for g in range(2):
                    lanes = slice(slot * 256 + g * 128, slot * 256 + g * 128 + 128)
                    tiles = swap_blocks([rows[8 * a : 8 * a + 8, lanes] for a in range(4)])
                    for q in range(4):
                        sb2[r * 16 + 2 * (4 * g + q) + place(slot)] = tiles[q].astype(BF16)
            send_row(sb2, rb2, 1, dr, r, 1 if first and i == 0 else 0)

    def mixed_group(step, carry):
        send_mixed(step * SPAN, False)
        return carry

    send_mixed(0, True)
    rb2[me] = sb2[me]
    lax.fori_loop(1, 8 // SPAN, mixed_group, 0)

    loads[2].wait()
    loads[3].wait()
    ow_t[...] = out_weight[...].astype(F32).T.astype(BF16)
    for s in range(8):
        lanes = pl.ds(s * 128, 128)
        gate = jax.nn.sigmoid(dot(w_t[pl.ds(512, 128)], normed[:, lanes]))
        gates[4, :, lanes] = gate
        cotangent = out_grad[:, s].reshape(128, 128).astype(F32).T
        og_t[:, lanes] = cotangent
        gpo = (cotangent * gate).astype(BF16)
        grad_po[:, lanes] = gpo
        grad_no[:, lanes] = dot(out_weight[...], gpo)

    arrive(rb2, 1)

    wide[:, 0:8, :] = rb2[...].astype(F32)
    gain_sum = jnp.zeros((128, 128), F32)
    for s in range(8):
        lanes = pl.ds(s * 128, 128)
        x = wide[:, s, :]
        centred = x - jnp.mean(x, axis=0, keepdims=True)
        rstd = lax.rsqrt(jnp.mean(centred * centred, axis=0, keepdims=True) + EPS)
        hat = centred * rstd
        gno = grad_no[:, lanes]
        gain_sum = gain_sum + gno * hat
        cot = gno * g_out[...]
        inner = jnp.mean(cot * hat, axis=0, keepdims=True)
        grad = rstd * (cot - jnp.mean(cot, axis=0, keepdims=True) - hat * inner)
        grad_no[:, lanes] = hat
        wide[:, 8 + s, :] = grad
    sb3[...] = wide[:, 8:16, :].astype(BF16)
    exchange(sb3, rb3, 2)

    def grad_rows(dr):
        r = lax.rem(rx + 8 - dr, 8)
        for slot in range(2):
            parts = []
            for g in range(2):
                parts.append(
                    swap_blocks([rb3[r * 16 + 2 * (4 * g + q) + place(slot)].astype(F32) for q in range(4)])
                )
            rows = [jnp.concatenate([parts[0][a], parts[1][a]], axis=1) for a in range(4)]
            grad_mat[slot, r] = jnp.concatenate(rows, axis=0).astype(BF16)
        to_sibling(grad_mat.at[1, r], grad_far.at[r], 2).start()

    def send_left(start, first):
        near = [(start + i, behind(start + i)) for i in range(SPAN)]
        for i, (dr, r) in enumerate(near):
            drain(sb3, 15 if first and i == 0 else 16, recv.at[2, dr])
            grad_rows(dr)
        every = sum(
            dot(jnp.concatenate([grad_mat[slot, r] for _, r in near], axis=0), side_of(slot, 1))
            for slot in range(2)
        )
        for i, (dr, r) in enumerate(near):
            rows = every[32 * i : 32 * i + 32]
            for g in range(4):
                tiles = swap_blocks([rows[8 * a : 8 * a + 8, g * 128 : g * 128 + 128] for a in range(4)])
                for q in range(4):
                    sb4[r * 16 + 4 * g + q] = tiles[q].astype(BF16)
            send_row(sb4, rb4, 3, dr, r, 1 if first and i == 0 else 0)

    def left_rows(step, carry):
        send_left(step * SPAN, False)
        return carry

    send_left(0, True)
    rb4[me] = sb4[me]
    lax.fori_loop(1, 8 // SPAN, left_rows, 0)
    to_sibling(edges.at[0, 0], edges.at[1, 0], 0).wait_recv()
    mine = grad_mat[0].reshape(256, 256)
    grad_right = dot(mine, side_of(0, 0), TN)
    to_sibling(grad_mat.at[1], grad_far, 2).wait_recv()
    grad_right = (grad_right + dot(grad_far[...].reshape(256, 256), side_of(1, 0), TN)).reshape(8, 4, 8, 512)
    for g in range(4):
        tiles = swap_blocks([grad_right[:, a, :, g * 128 : g * 128 + 128] for a in range(4)])
        for q in range(4):
            sb6.reshape(8, 16, 8, 128)[:, 4 * g + q] = tiles[q].astype(BF16)
    exchange(sb6, rb6, 7)

    gain_out_part = jnp.sum(gain_sum.T, axis=0, keepdims=True)
    for s in range(8):
        lanes = pl.ds(s * 128, 128)
        no = (grad_no[:, lanes] * g_out[...]).astype(BF16)
        grad_p[pl.ds(0, 128), lanes] = no
        po = dot(ow_t[...], no)
        gate = gates[4, :, lanes]
        update_o[:, s] = (gate * po).T.reshape(4, 32, 128).astype(BF16)
        grad_p[pl.ds(512, 128), lanes] = (og_t[:, lanes] * po * (gate * (1.0 - gate))).astype(BF16)
    out_part = dot(grad_p[pl.ds(0, 128)], grad_po[...], NT)
    gate_part = dot(normed[...], grad_p[pl.ds(512, 128)], NT)
    sums[:, 4, :] = gate_part
    sums[:, 5, :] = out_part
    sums[:, 7, :] = jnp.broadcast_to(gain_out_part, (128, 128))

    def edge_grads(buffer, gate, r):
        first = pl.multiple_of(r * 16, 16)
        here = pl.ds(first, 16)
        wide[here, 0:8, :] = buffer[here].astype(F32)
        for s in range(8):
            lanes = pl.ds(s * 128, 128)
            sig, value = gates[gate, here, lanes], gates[gate + 1, here, lanes]
            grad = wide[here, s, :] * sig
            grad_p[pl.ds(128 * gate + first, 16), lanes] = (grad * value * (1.0 - sig)).astype(BF16)
            grad_p[pl.ds(128 * gate + 128 + first, 16), lanes] = grad.astype(BF16)

    def left_group(dr, carry):
        drain(rb4, 16, recv.at[3, dr])
        edge_grads(rb4, 0, lax.rem(rx + dr, 8))
        return carry

    def right_group(dr, carry):
        drain(rb6, 16, recv.at[7, dr])
        edge_grads(rb6, 2, lax.rem(rx + 8 - dr, 8))
        return carry

    drain(rb4, 15, recv.at[3, 0])
    edge_grads(rb4, 0, rx)
    lax.fori_loop(1, 8, left_group, 0)
    for s in range(8):
        lanes = pl.ds(s * 128, 128)
        og_t[:, lanes] = dot(weight[:, 0:256], grad_p[pl.ds(0, 256), lanes]) + dot(
            weight[:, 512:640], grad_p[pl.ds(512, 128), lanes]
        )
    in_part = dot(normed[...], grad_p[pl.ds(0, 256)], NT)
    for b in range(2):
        sums[:, b, :] = in_part[:, b * 128 : b * 128 + 128]
    drain(rb6, 15, recv.at[7, 0])
    edge_grads(rb6, 2, rx)
    lax.fori_loop(1, 8, right_group, 0)
    gain_sum = jnp.zeros((128, 128), F32)
    for s in range(8):
        lanes = pl.ds(s * 128, 128)
        gni = og_t[:, lanes] + dot(weight[:, 256:512], grad_p[pl.ds(256, 256), lanes])
        gain_sum = gain_sum + gni * hat_in[:, lanes]
        og_t[:, lanes] = gni
    gain_in_part = jnp.sum(gain_sum.T, axis=0, keepdims=True)
    in_part = dot(normed[...], grad_p[pl.ds(256, 256)], NT)
    for b in range(2):
        sums[:, 2 + b, :] = in_part[:, b * 128 : b * 128 + 128]
    sums[:, 6, :] = jnp.broadcast_to(gain_in_part, (128, 128))

    def along_plane(source, target, slot):
        def one(d, carry):
            p, device = in_plane(d)
            pltpu.make_async_remote_copy(
                src_ref=source(p), dst_ref=target, send_sem=send.at[slot], recv_sem=recv.at[slot, 0],
                device_id=device, device_id_type=MESH,
            ).start()
            return carry

        lax.fori_loop(1, 32, one, 0, unroll=True)

    def rows_of(p):
        return pl.ds(pl.multiple_of(p * 4, 4), 4)

    sb5[...] = sums[...].astype(BF16)
    along_plane(lambda p: sb5.at[rows_of(p)], rb5.at[spot], 4)
    rb5[spot] = sb5[rows_of(spot)]
    for s in range(8):
        lanes = pl.ds(s * 128, 128)
        hat = hat_in[:, lanes]
        cot = og_t[:, lanes] * g_in[...]
        inner = jnp.mean(cot * hat, axis=0, keepdims=True)
        grad = rstd_in[:, lanes] * (cot - jnp.mean(cot, axis=0, keepdims=True) - hat * inner)
        pair_grad_o[:, s] = grad.T.reshape(4, 32, 128)
    drain(rb5, 31, recv.at[4, 0])
    plane_sum[...] = jnp.sum(rb5[...].astype(F32), axis=0).astype(BF16)

    def along_z(d, carry):
        pltpu.make_async_remote_copy(
            src_ref=plane_sum, dst_ref=planes.at[z], send_sem=send.at[5], recv_sem=recv.at[5, 0],
            device_id=(row, lax.div(col, 8) * 8 + lax.rem(z + d, 8)), device_id_type=MESH,
        ).start()
        return carry

    lax.fori_loop(1, 8, along_z, 0, unroll=True)
    planes[z] = plane_sum[...]
    drain(planes, 7, recv.at[5, 0])
    total = jnp.sum(planes[...].astype(F32), axis=0)
    gain_grad_o[...] = total[0, 6:8]
    total_bf[...] = total.astype(BF16)
    along_plane(lambda p: total_bf, final.at[rows_of(spot)], 6)
    final[rows_of(spot)] = total_bf[...]
    drain(sb1, 127, send.at[0])
    drain(sb0, 127, send.at[8])
    drain(rb2, 127, send.at[1])
    drain(sb3, 127, send.at[2])
    drain(rb4, 127, send.at[3])
    drain(rb6, 127, send.at[7])
    drain(rb5, 31, send.at[4])
    drain(planes, 7, send.at[5])
    drain(rb5, 31, send.at[6])
    for side in range(2):
        to_sibling(edges.at[0, side], edges.at[1, side], side).wait_send()
    to_sibling(grad_mat.at[1], grad_far, 2).wait_send()
    drain(rb5, 31, recv.at[6, 0])
    sums[...] = final[...].astype(F32)
    for b in range(5):
        weight_grad_o[:, pl.ds(b * 128, 128)] = sums[:, b, :]
    out_weight_grad_o[...] = sums[:, 5, :]


def write_out(*refs):
    count = len(refs) // 2
    copies = [
        pltpu.make_async_copy(refs[i], refs[count + i], refs[-1].at[i]) for i in range(count)
    ]
    for copy in copies:
        copy.start()
    for copy in copies:
        copy.wait()


def on_device(pair, gain_in, in_weight, gain_out, out_weight, out_grad):
    vmem = pl.BlockSpec(memory_space=pltpu.VMEM)
    hbm = pl.BlockSpec(memory_space=pltpu.HBM)
    scratch = [
        ((4, 8, 32, 128), BF16),
        ((128, 640), BF16),
        ((128, 128), BF16),
        ((4, 8, 32, 128), BF16),
        ((1, 128), F32),
        ((1, 128), F32),
        ((128, 16, 128), F32),
        ((128, 8, 128), BF16),
        ((128, 8, 128), BF16),
        ((128, 8, 128), BF16),
        ((128, 8, 128), BF16),
        ((2, 2, 8, 32, 512), BF16),
        ((512, 512), BF16),
        ((128, 8, 128), BF16),
        ((128, 8, 128), BF16),
        ((128, 8, 128), BF16),
        ((128, 8, 128), BF16),
        ((2, 8, 32, 256), BF16),
        ((8, 32, 256), BF16),
        ((128, 8, 128), BF16),
        ((128, 8, 128), BF16),
        ((128, 8, 128), BF16),
        ((128, 8, 128), BF16),
        ((128, 1024), BF16),
        ((128, 1024), F32),
        ((1, 1024), F32),
        ((5, 128, 1024), F32),
        ((128, 1024), BF16),
        ((128, 1024), F32),
        ((128, 1024), F32),
        ((640, 1024), BF16),
        ((640, 128), BF16),
        ((128, 128), BF16),
        ((128, 128), F32),
        ((128, 128), F32),
        ((128, 8, 128), BF16),
        ((32, 4, 8, 128), BF16),
        ((128, 8, 128), F32),
        ((4, 8, 128), BF16),
        ((8, 4, 8, 128), BF16),
        ((4, 8, 128), BF16),
        ((128, 8, 128), BF16),
    ]
    shapes = (
        jax.ShapeDtypeStruct((4, 8, 32, 128), BF16),
        jax.ShapeDtypeStruct((4, 8, 32, 128), F32),
        jax.ShapeDtypeStruct((128, 640), F32),
        jax.ShapeDtypeStruct((128, 128), F32),
        jax.ShapeDtypeStruct((2, 128), F32),
    )
    operands = [
        pltpu.with_memory_space_constraint(value, pltpu.HBM)
        for value in (
            pair.reshape(4, 8, 32, 128), gain_in.reshape(1, 128), in_weight,
            gain_out.reshape(1, 128), out_weight, out_grad.reshape(4, 8, 32, 128),
        )
    ]
    results = pl.pallas_call(
        kernel,
        out_shape=shapes,
        in_specs=[hbm] * 6,
        out_specs=[vmem] * 5,
        scratch_shapes=[pltpu.VMEM(shape, kind) for shape, kind in scratch]
        + [
            pltpu.SemaphoreType.DMA((6,)),
            pltpu.SemaphoreType.DMA((9,)),
            pltpu.SemaphoreType.DMA((9, 8)),
            pltpu.SemaphoreType.DMA((3,)),
            pltpu.SemaphoreType.DMA((3,)),
        ],
        compiler_params=pltpu.CompilerParams(
            collective_id=0, has_side_effects=True, vmem_limit_bytes=48 * 2**20
        ),
    )(*operands)
    update, pair_grad, in_weight_grad, out_weight_grad, gain_grad = pl.pallas_call(
        write_out,
        out_shape=shapes,
        in_specs=[vmem] * 5,
        out_specs=[hbm] * 5,
        scratch_shapes=[pltpu.SemaphoreType.DMA((5,))],
        compiler_params=pltpu.CompilerParams(vmem_limit_bytes=16 * 2**20),
    )(*results)
    return (
        update.reshape(32, 32, 128), pair_grad.reshape(32, 32, 128),
        in_weight_grad, out_weight_grad, gain_grad,
    )


def solution(mesh):
    return jax.shard_map(
        on_device,
        mesh=mesh,
        in_specs=(P("row", "col", None), P(), P(), P(), P(), P("row", "col", None)),
        out_specs=(P("row", "col", None), P("row", "col", None), P(), P(), P()),
        check_vma=False,
    )
```
